32 devices in a mesh: expert: 8 (over z, y), ctx: 4 (over x, core).
Axes of the slice: x: 2, y: 2, z: 4, core: 2. Of those that a mesh axis runs over, the one named last changes fastest.
Arguments:
- tokens: bfloat16 [1024, 4096], P('expert', 'ctx'), may hold values from -6 to 6
- grad_out: bfloat16 [1024, 4096], P('expert', 'ctx'), may hold values from -1.5 to 1.5
- expert_ids: int32 [1024, 8], P('expert'), may hold values from 0 to 15, all different within a row; in each aligned block of 128 rows (0 to 127, 128 to 255, ...) at most 72 rows name the same one
- gate_probs: float32 [1024, 8], P('expert'), may hold values from 0.05 to 1
- gate_weight: bfloat16 [16, 1536, 4096], P('expert', 'ctx'), may hold values from -0.09375 to 0.09375
- up_weight: bfloat16 [16, 1536, 4096], P('expert', 'ctx'), may hold values from -0.09375 to 0.09375
- down_weight: bfloat16 [16, 1536, 4096], P('expert', 'ctx'), may hold values from -0.15625 to 0.15625
Outputs:
- grad_tokens: bfloat16 [1024, 4096], P('expert', 'ctx')
- grad_gates: bfloat16 [1024, 8], P('expert')
The draws below stay inside these ranges and needn't reach their ends.
Inputs may be any that keep to these rules, and one draw needn't show every extreme that they name: `expert_ids`: each row names 8 different experts. Within the 128 rows of one index of expert (aligned blocks), no expert is named more than 72 times, and in every draw some expert is named exactly 72 times in some block.
All inputs are finite; a program needn't handle non-finite values.
Results may differ from the reference program's by a relative error of at most 0.014.
Values may be sent and summed in bfloat16 or wider, within the bound.
No kernel may reach another device: no remote copies, remote signals or barrier semaphores. Data moves between devices by JAX's collectives and lax.ppermute only.
A program may use at most 128 MiB of HBM per device.

```python
import math
import jax
import jax.numpy as jnp
import numpy as np
from jax import lax

D = 4096
FF = 1536
TOP = 8
TOK_DEV = 128
EXPERTS = 16
TOKENS = 1024
CAP = 72
N_EXPERT = 8
N_CTX = 4


def block_scale(key, extent, split, smallest, high):
    loudness = 1.0
    for position, shards_of in split:
        draws = jax.random.uniform(jax.random.fold_in(jax.random.fold_in(key, 6), position), (shards_of,), jnp.float32, smallest / len(split), high / len(split))
        loudness = loudness * jnp.repeat(jnp.exp(draws), extent[position] // shards_of).reshape((-1,) + (1,) * (len(extent) - 1 - position))
    return loudness


def shared_out(key, own, number, rows, number_of, top, most, skew):
    sequence = jax.random.permutation(key, number_of)
    packed, usual = portions_of(number_of, rows * top, most, skew, True), portions_of(number_of, rows * top, most, skew, False)
    places = jnp.arange(number_of)

    def named(sizes, turn):
        used = int((sizes > 0).sum())
        fixed = max(1, used // 4)
        moved = fixed + (places - fixed + turn * (used - fixed)) % max(1, number_of - fixed)
        return jnp.zeros((number_of,), jnp.int32).at[sequence[jnp.where(places < fixed, places, moved)]].set(jnp.asarray(sizes, jnp.int32))

    sizes = jnp.where(number % 4 == 0, named(packed, number // 4), named(usual, number - number // 4 - 1))
    mixed = jax.random.permutation(jax.random.fold_in(own, 3), number_of)
    source_of, taker = mixed[0:number_of // 2 * 2:2], mixed[1:number_of // 2 * 2:2]
    margin = jnp.minimum(sizes[source_of] - 1, most - sizes[taker]) // 2
    margin = jnp.where((source_of == sequence[0]) | (taker == sequence[0]) | (sizes[taker] == 0), 0, jnp.maximum(margin, 0))
    moved = jax.random.randint(jax.random.fold_in(own, 4), (number_of // 2,), 0, 1 << 20) % (margin + 1)
    sizes = sizes.at[source_of].add(-moved).at[taker].add(moved)
    items = jnp.searchsorted(jnp.cumsum(sizes), jnp.arange(rows * top), side="right").astype(jnp.int32)
    grid = items.reshape(top, rows).T
    grid = grid[jax.random.permutation(jax.random.fold_in(own, 1), rows)]
    turn = jax.random.randint(jax.random.fold_in(own, 2), (rows, 1), 0, top)
    return jnp.take_along_axis(grid, (jnp.arange(top)[None, :] + turn) % top, axis=1)


def portions_of(count, total, reach, slope, full):
    loads = [(1 << 20) // math.isqrt(standing ** slope) + 1 for standing in range(1, count + 1)]
    largest = reach if full else min(reach, max(-(-total // count), total * loads[0] // sum(loads)))
    least = 1 if total - largest >= count - 1 else 0
    given, surplus = [largest] + [least] * (count - 1), total - largest - least * (count - 1)
    while surplus > 0:
        movable = [i for i in range(1, count) if given[i] < largest] or [i for i in range(1, count) if given[i] < reach]
        pool, remaining = sum([loads[i] for i in movable]), surplus
        for i in movable:
            addition = min(reach - given[i], max(1, remaining * loads[i] // pool), surplus)
            given[i] = given[i] + addition
            surplus = surplus - addition
    return np.array(given)


def centred(rng, extent, deviation, reach, pieces=(), held_as=jnp.bfloat16):
    result = deviation * jax.random.normal(rng, extent, jnp.float32)
    if pieces:
        result = result * block_scale(rng, extent, pieces, -0.22, 0.18)
    return jnp.clip(result, -reach, reach).astype(held_as)


def setup_inputs(seed: int = 0) -> dict:
    splits = jax.random.split(jax.random.key(seed), 8)
    tokens = centred(splits[0], (TOKENS, D), 1.0, 6.0, ((0, 8), (1, 4)))
    grad_out = centred(splits[1], (TOKENS, D), 0.25, 1.5, ((0, 8), (1, 4)))
    expert_ids_keys = jax.random.split(jax.random.fold_in(splits[2], 1), TOKENS // TOK_DEV)
    expert_ids_turns = jax.random.permutation(jax.random.fold_in(splits[2], 3), TOKENS // TOK_DEV)
    expert_ids = jax.vmap(lambda own, number: shared_out(jax.random.fold_in(splits[2], 2), own, number, TOK_DEV, EXPERTS, TOP, CAP, 0))(expert_ids_keys, expert_ids_turns).reshape((TOKENS, TOP))
    gate_probs = jnp.clip(jnp.exp(math.log(1.0) - 2.9957323 * jax.random.uniform(splits[3], (TOKENS, TOP), jnp.float32) ** block_scale(splits[3], (TOKENS, TOP), ((0, 8),), -0.2, 0.2)), 0.05, 1.0)
    gate_weight = centred(splits[4], (EXPERTS, FF, D), D ** -0.5, 0.09375, ((0, 8), (1, 4)))
    up_weight = centred(splits[5], (EXPERTS, FF, D), D ** -0.5, 0.09375, ((0, 8), (1, 4)))
    down_weight = centred(splits[6], (EXPERTS, FF, D), FF ** -0.5, 0.15625, ((0, 8), (1, 4)))
    return {"tokens": tokens, "grad_out": grad_out, "expert_ids": expert_ids, "gate_probs": gate_probs, "gate_weight": gate_weight, "up_weight": up_weight, "down_weight": down_weight}


def reference(tokens, grad_out, expert_ids, gate_probs, gate_weight, up_weight, down_weight):
    per_block = TOK_DEV * TOP
    row_count = N_EXPERT * CAP
    ff_block = FF // N_CTX
    blocks = expert_ids.reshape(N_EXPERT, per_block)
    one_hot = (blocks[:, :, None] == jnp.arange(EXPERTS, dtype=jnp.int32)[None, None, :]).astype(jnp.int32)
    earlier = jnp.cumsum(one_hot, axis=1) - one_hot
    slot_rank = jnp.sum(earlier * one_hot, axis=2).astype(jnp.int32)
    block_ids = jnp.broadcast_to(jnp.arange(N_EXPERT, dtype=jnp.int32)[:, None], (N_EXPERT, per_block))
    token_ids = (block_ids * TOK_DEV + jnp.arange(per_block, dtype=jnp.int32)[None, :] // TOP).astype(jnp.int32)
    columns = (block_ids * CAP + slot_rank).astype(jnp.int32)
    index_table = jnp.zeros((EXPERTS, row_count), jnp.int32).at[blocks, columns].set(token_ids)
    filled_table = jnp.zeros((EXPERTS, row_count), jnp.float32).at[blocks, columns].set(1.0)
    weight_table = jnp.zeros((EXPERTS, row_count), jnp.float32).at[blocks, columns].set(gate_probs.reshape(N_EXPERT, per_block))

    def expert_step(running, inputs_row):
        row_index, filled, gate_rows, gate_mat, up_mat, down_mat = inputs_row
        keep = filled[:, None] > 0.5
        rows_in = jnp.where(keep, tokens[row_index], jnp.zeros((), jnp.bfloat16))
        rows_grad = jnp.where(keep, grad_out[row_index], jnp.zeros((), jnp.bfloat16))
        pre_gate = jnp.dot(rows_in, gate_mat.T, preferred_element_type=jnp.float32)
        pre_up = jnp.dot(rows_in, up_mat.T, preferred_element_type=jnp.float32)
        grad_hidden = jnp.dot(rows_grad, down_mat.T, preferred_element_type=jnp.float32)
        sigmoid_gate = jax.nn.sigmoid(pre_gate)
        activated = pre_gate * sigmoid_gate
        gate_score = jnp.sum(activated * pre_up * grad_hidden, axis=1).astype(jnp.bfloat16)
        grad_pre_gate = (grad_hidden * pre_up * sigmoid_gate * (1.0 + pre_gate * (1.0 - sigmoid_gate))).astype(jnp.bfloat16)
        grad_pre_up = (grad_hidden * activated).astype(jnp.bfloat16)
        gpg = grad_pre_gate.astype(jnp.float32).reshape(row_count, N_CTX, ff_block)
        gpu = grad_pre_up.astype(jnp.float32).reshape(row_count, N_CTX, ff_block)
        gate_blocks = gate_mat.astype(jnp.float32).reshape(N_CTX, ff_block, D)
        up_blocks = up_mat.astype(jnp.float32).reshape(N_CTX, ff_block, D)
        block_terms = jnp.einsum("rcf,cfd->crd", gpg, gate_blocks) + jnp.einsum("rcf,cfd->crd", gpu, up_blocks)
        rounded = lax.optimization_barrier(block_terms.astype(jnp.bfloat16))
        combined = jnp.sum(rounded.astype(jnp.float32), axis=0).astype(jnp.bfloat16)
        added = gate_rows[:, None] * combined.astype(jnp.float32) * filled[:, None]
        return running.at[row_index].add(added), gate_score

    start = jnp.zeros((TOKENS, D), jnp.float32)
    running, scores = lax.scan(expert_step, start, (index_table, filled_table, weight_table, gate_weight, up_weight, down_weight))
    grad_gates = scores[blocks, columns].reshape(TOKENS, TOP)
    return running.astype(jnp.bfloat16), grad_gates
```

```python
import functools
import jax
import jax.numpy as jnp
from jax import lax
from jax.experimental import pallas as pl
from jax.experimental.pallas import tpu as pltpu
from jax.sharding import Mesh, PartitionSpec as P

NT = (((1,), (1,)), ((), ()))
NN = (((1,), (0,)), ((), ()))


def expert_kernel(plan, *refs):
    piece_at, out_at, n_in, n_q, ndy, ndx, local, tile, wide = plan
    where = refs[0]
    pieces = refs[1 : 1 + n_in]
    probs, wg_hbm, wu_hbm, wd_hbm = refs[1 + n_in : 5 + n_in]
    outs = refs[5 + n_in : 5 + n_in + 2 * n_q]
    score, wg, wu, wd, d_gate, d_up, w_sem = refs[5 + n_in + 2 * n_q :]
    rows, width = pieces[0].shape[1:]
    units = wg.shape[0]
    hidden = units // local
    tiles = units // tile
    slabs = [(q, dy) for q in range(n_q) for dy in range(ndy)]
    blocks = [(dx, dc) for dx in range(ndx) for dc in range(2)]

    def feature(dx, dc):
        return pl.multiple_of(where[1 + 2 * dx + dc] * width, width)

    def weight_copy(k, n):
        part = pl.ds(pl.multiple_of(n * tile, tile), tile)
        source, target = ((wg_hbm, wg), (wu_hbm, wu), (wd_hbm, wd))[k]
        return pltpu.make_async_copy(source.at[part], target.at[part], w_sem.at[k, n])

    for k in range(3):
        weight_copy(k, 0).start()

    def product(kind, ref, first):
        total = None
        for dx, dc in blocks:
            x = jnp.concatenate([pieces[piece_at[q][dy, dx, dc]][kind] for q, dy in slabs], axis=0)
            w = ref[pl.ds(first, tile), pl.ds(feature(dx, dc), width)]
            term = lax.dot_general(x, w, NT, preferred_element_type=jnp.float32)
            total = term if total is None else total + term
        return total

    column = lax.broadcasted_iota(jnp.int32, (rows, probs.shape[3]), 1)
    shares = []
    for e in range(local):
        mine = column == where[0] * local + e
        shares.append(
            jnp.concatenate(
                [
                    jnp.sum(jnp.where(mine, probs[q, dy], 0.0), axis=1, keepdims=True)
                    for q, dy in slabs
                ],
                axis=0,
            )
        )
    score[...] = jnp.zeros(score.shape, jnp.float32)
    score_lane = lax.broadcasted_iota(jnp.int32, score.shape, 1)

    @pl.loop(0, tiles)
    def _(n):
        first = pl.multiple_of(n * tile, tile)
        weight_copy(0, n).wait()

        @pl.when(n + 1 < tiles)
        def _():
            for k in range(3):
                weight_copy(k, n + 1).start()

        gate = product(0, wg, first)
        weight_copy(1, n).wait()
        up = product(0, wu, first)
        weight_copy(2, n).wait()
        hid = product(1, wd, first)
        unit = first + lax.broadcasted_iota(jnp.int32, gate.shape, 1)
        share = jnp.zeros(gate.shape, jnp.float32)
        sig = jax.nn.sigmoid(gate)
        act = gate * sig
        both = up * hid
        scores = act * both
        total = score[...]
        for e in range(local):
            inside = (unit >= e * hidden) & (unit < (e + 1) * hidden)
            share = jnp.where(inside, shares[e], share)
            own = jnp.sum(jnp.where(inside, scores, 0.0), axis=1, keepdims=True)
            total = total + jnp.where(score_lane == e, own, 0.0)
        score[...] = total
        d_gate[:, pl.ds(first, tile)] = (share * (both * sig * (1.0 + gate * (1.0 - sig)))).astype(
            jnp.bfloat16
        )
        d_up[:, pl.ds(first, tile)] = (share * (hid * act)).astype(jnp.bfloat16)

    for dx, dc in blocks:
        @pl.loop(0, width // wide)
        def _(n):
            at = pl.multiple_of(n * wide, wide)
            source = pl.ds(pl.multiple_of(feature(dx, dc) + at, wide), wide)
            total = lax.dot_general(
                d_gate[...], wg[:, source], NN, preferred_element_type=jnp.float32
            ) + lax.dot_general(d_up[...], wu[:, source], NN, preferred_element_type=jnp.float32)
            total = total.astype(jnp.bfloat16)
            for i, (q, dy) in enumerate(slabs):
                outs[2 * q + dc][out_at[q][dy, dx], :, pl.ds(at, wide)] = total[i * rows : (i + 1) * rows]


def expert_call(where, pieces, probs, wg, wu, wd, local, piece_at, out_at, ndy, ndx):
    units, full = wg.shape
    rows, width = pieces[0][0].shape[1:]
    tile = next(t for t in (256, 128, 64, 32, 16) if units % t == 0)
    wide = next(t for t in (1024, 512, 256, 128) if width % t == 0)
    vmem, hbm = pl.BlockSpec(memory_space=pltpu.VMEM), pl.BlockSpec(memory_space=pltpu.HBM)
    out = jax.ShapeDtypeStruct((ndy * ndx, rows, width), jnp.bfloat16)
    n_q, first = len(pieces), 0
    places = []
    for at, of in zip(piece_at, pieces):
        places.append({l: first + i for l, i in at.items()})
        first += len(of)
    plan = (places, out_at, first, n_q, ndy, ndx, local, tile, wide)
    weight = pltpu.VMEM((units, full), jnp.bfloat16)
    m = n_q * ndy * rows
    results = pl.pallas_call(
        functools.partial(expert_kernel, plan),
        in_specs=[pl.BlockSpec(memory_space=pltpu.SMEM)] + [vmem] * (first + 1) + [hbm] * 3,
        out_specs=[vmem] * (2 * n_q + 1),
        scratch_shapes=[weight] * 3
        + [pltpu.VMEM((m, units), jnp.bfloat16)] * 2
        + [pltpu.SemaphoreType.DMA((3, units // tile))],
        out_shape=[out] * (2 * n_q) + [jax.ShapeDtypeStruct((m, 128), jnp.float32)],
        compiler_params=pltpu.CompilerParams(vmem_limit_bytes=40 << 20),
        cost_estimate=pl.CostEstimate(
            flops=10 * m * units * full, bytes_accessed=6 * units * full, transcendentals=0
        ),
    )(where, *[p for of in pieces for p in of], probs, *[
        pltpu.with_memory_space_constraint(w, pltpu.HBM) for w in (wg, wu, wd)
    ])
    return [results[2 * q : 2 * q + 2] for q in range(n_q)], results[-1]


def exchange(x, axis, step):
    return lax.ppermute(x, axis, [(i, i ^ step) for i in range(lax.axis_size(axis))])


def bits(size):
    return [1 << b for b in range(size.bit_length() - 1)]


def last_bit(v):
    return 1 << (v.bit_length() - 1)


def added(a, b):
    return (a.astype(jnp.float32) + b.astype(jnp.float32)).astype(jnp.bfloat16)


def body(tokens, grad_out, expert_ids, gate_probs, gate_weight, up_weight, down_weight):
    far, near, cols = lax.axis_size("far"), lax.axis_size("near"), lax.axis_size("col")
    z, y, x, c = (lax.axis_index(n) for n in ("far", "near", "col", "half"))
    me = z * near + y
    local, _, full = gate_weight.shape
    weights = [w.reshape(-1, full) for w in (gate_weight, up_weight, down_weight)]
    experts = local * far * near
    rows, width = tokens.shape
    spread = jax.nn.one_hot(expert_ids, experts, dtype=jnp.float32)
    probs = jnp.sum(spread * gate_probs[:, :, None], axis=1)
    features = [(x ^ dx) * 2 + (c ^ dc) for dx in range(cols) for dc in range(2)]
    where = jnp.stack([me] + features).astype(jnp.int32)
    labels = [(dy, dx) for dy in range(near) for dx in range(cols)]
    depth = {l: bin(l[0]).count("1") + bin(l[1]).count("1") for l in labels}
    depths = max(depth.values())

    have = [{} for _ in range(far)]
    have[0][0, 0, 0] = jnp.stack([tokens, grad_out])
    scores = [None] * far

    def level_ops(q, level):
        ops = []
        for dy, dx in labels:
            if depth[dy, dx] != level:
                continue
            if dy and (q % 2 == 0 or not dx):
                ops.append((q, (dy, dx, 0), (dy ^ last_bit(dy), dx, 0), "near", last_bit(dy)))
            else:
                ops.append((q, (dy, dx, 0), (dy, dx ^ last_bit(dx), 0), "col", last_bit(dx)))
        return sorted(ops, key=lambda o: o[3])

    def half_ops(q, levels):
        return [(q, (dy, dx, 1), (dy, dx, 0), "half", 1) for dy, dx in labels if depth[dy, dx] in levels]

    def far_ops(q):
        return [(q, (0, 0, 0), None, "far", q)] if 0 < q < far else []

    def tied(values, ready):
        return lax.optimization_barrier((values, ready))[0] if ready else values

    def run(ops, ready):
        sources = [have[0][0, 0, 0] if o[2] is None else have[o[0]][o[2]] for o in ops]
        for o, a in zip(ops, tied(sources, ready)):
            have[o[0]][o[1]] = exchange(a, o[3], o[4])
        return [have[o[0]][o[1]] for o in ops if o[3] in ("near", "col")]

    def compute(qs, ready):
        pieces = [list(have[q].values()) for q in qs]
        piece_at = [{l: i for i, l in enumerate(have[q])} for q in qs]
        out_at = []
        for q in qs:
            x_major = q % 2 == 1
            out_at.append({(dy, dx): dx * near + dy if x_major else dy * cols + dx for dy, dx in labels})
        table = tied(jnp.stack([both[q] for q in qs]), ready)
        outs, score = expert_call(where, pieces, table, *weights, local, piece_at, out_at, near, cols)
        for i, q in enumerate(qs):
            scores[q] = score[i * near * rows : (i + 1) * near * rows]
        return outs

    class Sum:
        def __init__(self, q, keep, send):
            self.q, self.keep = q, keep
            axes = ("col", "near") if q % 2 == 1 else ("near", "col")
            self.steps = [(a, s) for a in axes for s in reversed(bits(near if a == "near" else cols))]
            self.got = exchange(send, "half", 1)

        def fold(self):
            half = self.keep.shape[0] // 2
            self.send = added(self.keep[half:], self.got[half:])
            self.keep = added(self.keep[:half], self.got[:half])
            return [self.send, self.keep]

        def step(self, ready=()):
            axis, step = self.steps.pop(0)
            self.got = exchange(tied(self.send, list(ready)), axis, step)

        def home(self):
            mine = added(self.keep[0], self.got[0])
            return exchange(mine, "far", self.q) if self.q else mine

    table = [probs] + [exchange(probs, "far", q) for q in range(1, far)]
    both, done = None, []

    def group(ops, extra=()):
        ready = (done[-2] if len(done) > 1 else []) + list(extra)
        done.append(run(ops, ready))

    sums, total = [], None

    def finish(s):
        nonlocal total
        mine = s.home().astype(jnp.float32)
        total = mine if total is None else total + mine

    waiting, late = [], []
    for p in range(0, far, 2):
        a, b = p, p + 1
        if p == 0:
            group(far_ops(1) + far_ops(2) + level_ops(0, 1))
            group(far_ops(3) + level_ops(1, 1) + half_ops(0, (0,)), have[1].values())
            both = jnp.stack(table)
            group(level_ops(a, 2) + half_ops(a, (1,)), [both])
            both = jnp.stack([both, exchange(both, "near", 1)], axis=1)
            group(level_ops(b, 2) + half_ops(b, (0, 1)), list(have[2].values()) if far > 2 else [])
        else:
            group(level_ops(a, 1) + half_ops(a, (0,)) + late[: len(late) // 2] + far_ops(a + 2), [both])
            group(level_ops(b, 1) + half_ops(b, (0,)) + late[len(late) // 2 :] + far_ops(b + 2))
            late = []
            outs = compute(waiting, [])
            sums = [Sum(q, *o) for q, o in zip(waiting, outs)]
            waiting = []
            group(level_ops(a, 2) + half_ops(a, (1,)), sum(map(list, outs), []))
            group(level_ops(b, 2) + half_ops(b, (1,)), have[a + 2].values() if a + 2 < far else ())
        for level in range(3, depths + 1):
            group(level_ops(a, level) + half_ops(a, (level - 1,)))
            group(level_ops(b, level) + half_ops(b, (level - 1,)))
        late = half_ops(a, (depths,)) + half_ops(b, (depths,))
        waiting = [a, b]
        if sums and p + 2 < far:
            folded = [s.fold() for s in sums]
            while sums[0].steps:
                for s in sums:
                    s.step()
                if sums[0].steps:
                    for s in sums:
                        s.fold()
            for s in sums:
                finish(s)
            sums = []
    run(late, [])
    folded = sum([s.fold() for s in sums], [])
    for s in sums:
        s.step()
    first = Sum(waiting[0], *compute(waiting[:1], folded)[0])
    folded = sum([s.fold() for s in sums], [])
    for s in sums:
        s.step()
    folded += first.fold()
    first.step()
    second = Sum(waiting[1], *compute(waiting[1:], folded)[0])
    rest = sums + [first, second]
    second.fold()
    second.step()
    while rest:
        for s in list(rest):
            if s.steps:
                s.fold()
                s.step()
            else:
                finish(s)
                rest.remove(s)
    grad_tokens = total.astype(jnp.bfloat16)

    table = jnp.stack([s.reshape(near, rows, -1)[:, :, :local] for s in scores])
    table = table.transpose(0, 1, 3, 2)
    table = table + exchange(table, "half", 1)
    for step in bits(cols):
        table = table + exchange(table, "col", step)
    parts = [[table[q, dy] if dy == 0 else None for dy in range(near)] for q in range(far)]
    for dy in range(1, near):
        got = exchange(table[:, dy], "near", dy)
        for q in range(far):
            parts[q][dy] = got[q]
    for q in range(1, far):
        got = exchange(jnp.stack(parts[q]), "far", q)
        parts[q] = [got[dy] for dy in range(near)]
    found = jnp.stack([p for of in parts for p in of])
    index = jnp.arange(far * near)
    mine = (index[:, None] ^ me) == index[None, :]
    by_expert = jnp.sum(jnp.where(mine[:, :, None, None], found[None], 0.0), axis=1)
    by_expert = by_expert.reshape(experts, rows)
    grad_gates = jnp.sum(spread * by_expert.T[:, None, :], axis=2)
    return (grad_tokens, grad_gates.astype(jnp.bfloat16))


def solution(mesh):
    expert, ctx = mesh.shape["expert"], mesh.shape["ctx"]
    fine = Mesh(mesh.devices.reshape(expert // 2, 2, ctx // 2, 2), ("far", "near", "col", "half"))
    e, c = ("far", "near"), ("col", "half")
    return jax.shard_map(
        body,
        mesh=fine,
        in_specs=(P(e, c), P(e, c), P(e), P(e), P(e, c), P(e, c), P(e, c)),
        out_specs=(P(e, c), P(e)),
        check_vma=False,
    )
```

```python
import functools
import jax
import jax.numpy as jnp
from jax import lax
from jax.experimental import pallas as pl
from jax.experimental.pallas import tpu as pltpu
from jax.sharding import Mesh, PartitionSpec as P

NT = (((1,), (1,)), ((), ()))
NN = (((1,), (0,)), ((), ()))
TN = (((0,), (0,)), ((), ()))


def padded(count):
    return 16 * -(-count // 16)


def expert_kernel(plan, *refs):
    at, out_at, n_in, ndy, ndx, local, experts, rows, tile, wide = plan
    where = refs[0]
    pieces = refs[1 : 1 + n_in]
    wg, wu, wd, keep, send, d_gate, d_up, score = refs[1 + n_in :]
    width = pieces[0].shape[1]
    units = wg.shape[0]
    hidden = units // local
    blocks = [(dx, dc) for dx in range(ndx) for dc in range(2)]

    def feature(dx, dc):
        return pl.multiple_of(where[1 + 2 * dx + dc] * width, width)

    def part(kind, dy, dx, dc):
        ref, first = at[kind, dy, dx, dc]
        return pieces[ref][first : first + rows]

    def product(kind, ref, first):
        total = None
        for dx, dc in blocks:
            x = jnp.concatenate([part(kind, dy, dx, dc) for dy in range(ndy)], axis=0)
            w = ref[pl.ds(first, tile), pl.ds(feature(dx, dc), width)]
            term = lax.dot_general(x, w, NT, preferred_element_type=jnp.float32)
            total = term if total is None else total + term
        return total

    slots = padded(experts)
    expert = lax.broadcasted_iota(jnp.int32, (slots, 128), 0)
    column = lax.broadcasted_iota(jnp.int32, (slots, 128), 1)
    mine = jnp.where((expert == where[0] * local + column) & (column < local), 1.0, 0.0).astype(jnp.bfloat16)
    shares = []
    for dy in range(ndy):
        ref, first = at[2, dy, 0, 0]
        table = pieces[ref][first : first + slots]
        shares.append(
            sum(
                lax.dot_general(
                    table[:, i * rows : (i + 1) * rows], mine, TN, preferred_element_type=jnp.float32
                )
                for i in range(3)
            )
        )
    shares = jnp.concatenate(shares, axis=0)
    score[...] = jnp.zeros(score.shape, jnp.float32)

    @pl.loop(0, units // tile)
    def _(n):
        first = pl.multiple_of(n * tile, tile)
        gate, up, hid = product(0, wg, first), product(0, wu, first), product(1, wd, first)
        unit = first + lax.broadcasted_iota(jnp.int32, gate.shape, 1)
        share = jnp.zeros(gate.shape, jnp.float32)
        sig = jax.nn.sigmoid(gate)
        act = gate * sig
        both = up * hid
        scores = act * both
        for e in range(local):
            inside = (unit >= e * hidden) & (unit < (e + 1) * hidden)
            share = jnp.where(inside, shares[:, e : e + 1], share)
        row = lax.broadcasted_iota(jnp.int32, (score.shape[0], tile), 0) * hidden
        of = first + lax.broadcasted_iota(jnp.int32, (score.shape[0], tile), 1)
        pick = jnp.where((of >= row) & (of < row + hidden), 1.0, 0.0).astype(jnp.bfloat16)
        high = scores.astype(jnp.bfloat16)
        low = (scores - high.astype(jnp.float32)).astype(jnp.bfloat16)
        score[...] += lax.dot_general(pick, high, NT, preferred_element_type=jnp.float32) + lax.dot_general(
            pick, low, NT, preferred_element_type=jnp.float32
        )
        d_gate[:, pl.ds(first, tile)] = (share * (both * sig * (1.0 + gate * (1.0 - sig)))).astype(
            jnp.bfloat16
        )
        d_up[:, pl.ds(first, tile)] = (share * (hid * act)).astype(jnp.bfloat16)

    extra = keep.shape[1] - rows
    per_row = width // rows
    place = lax.broadcasted_iota(jnp.int32, (extra, width), 0) * per_row
    place = place + lax.broadcasted_iota(jnp.int32, (extra, width), 1) // rows
    for dy in range(ndy):
        table = jnp.zeros((extra, width), jnp.float32)
        for e in range(local):
            line = jnp.concatenate([score[e : e + 1, dy * rows : (dy + 1) * rows]] * per_row, axis=1)
            table = jnp.where(place == where[0] * local + e, line, table)
        for dx, dc in blocks:
            (keep, send)[dc][out_at[dy, dx], rows:, :] = table.astype(jnp.bfloat16)

    for dx, dc in blocks:

        @pl.loop(0, width // wide)
        def _(n):
            start = pl.multiple_of(n * wide, wide)
            source = pl.ds(pl.multiple_of(feature(dx, dc) + start, wide), wide)
            total = lax.dot_general(
                d_gate[...], wg[:, source], NN, preferred_element_type=jnp.float32
            ) + lax.dot_general(d_up[...], wu[:, source], NN, preferred_element_type=jnp.float32)
            total = total.astype(jnp.bfloat16)
            for dy in range(ndy):
                (keep, send)[dc][out_at[dy, dx], :rows, pl.ds(start, wide)] = total[dy * rows : (dy + 1) * rows]


def expert_call(where, pieces, weights, local, experts, rows, at, out_at, ndy, ndx):
    units, full = weights[0].shape
    width = pieces[0].shape[1]
    tile = next(t for t in (256, 128, 64, 32, 16) if units % t == 0)
    wide = next(t for t in (1024, 512, 256, 128) if width % t == 0)
    vmem = pl.BlockSpec(memory_space=pltpu.VMEM)
    extra = padded(-(-experts // (width // rows)))
    out = jax.ShapeDtypeStruct((ndy * ndx, rows + extra, width), jnp.bfloat16)
    m = ndy * rows
    return pl.pallas_call(
        functools.partial(
            expert_kernel, (at, out_at, len(pieces), ndy, ndx, local, experts, rows, tile, wide)
        ),
        in_specs=[pl.BlockSpec(memory_space=pltpu.SMEM)] + [vmem] * (len(pieces) + 3),
        out_specs=[vmem] * 2,
        scratch_shapes=[pltpu.VMEM((m, units), jnp.bfloat16)] * 2
        + [pltpu.VMEM((padded(local), m), jnp.float32)],
        out_shape=[out] * 2,
        compiler_params=pltpu.CompilerParams(vmem_limit_bytes=16 << 20),
        cost_estimate=pl.CostEstimate(
            flops=10 * m * units * full, bytes_accessed=6 * units * full, transcendentals=0
        ),
    )(where, *pieces, *weights)


def exchange(x, axis, step):
    return lax.ppermute(x, axis, [(i, i ^ step) for i in range(lax.axis_size(axis))])


def passed(x, axis, pairs):
    return lax.ppermute(x, axis, pairs)


def bits(size):
    return [1 << b for b in range(size.bit_length() - 1)]


def last_bit(v):
    return 1 << (v.bit_length() - 1)


def added(a, b):
    return (a.astype(jnp.float32) + b.astype(jnp.float32)).astype(jnp.bfloat16)


class Cell:
    def __init__(self, value):
        self.v = value


def together(cells):
    cells = list({id(c): c for c in cells}.values())
    if len(cells) > 1:
        for c, v in zip(cells, lax.optimization_barrier([c.v for c in cells])):
            c.v = v


def touch_kernel(where, *refs):
    for i in range(where.shape[0]):
        refs[-1][i] = where[i]


def touch_call(where, arrays):
    smem, vmem = pl.BlockSpec(memory_space=pltpu.SMEM), pl.BlockSpec(memory_space=pltpu.VMEM)
    return pl.pallas_call(
        touch_kernel,
        in_specs=[smem] + [vmem] * len(arrays),
        out_specs=smem,
        out_shape=jax.ShapeDtypeStruct(where.shape, where.dtype),
        compiler_params=pltpu.CompilerParams(vmem_limit_bytes=2 << 20),
    )(where, *arrays)


def body(tokens, grad_out, expert_ids, gate_probs, gate_weight, up_weight, down_weight):
    far, near, cols = lax.axis_size("far"), lax.axis_size("near"), lax.axis_size("col")
    z, y, x, c = (lax.axis_index(n) for n in ("far", "near", "col", "half"))
    me = z * near + y
    local, _, full = gate_weight.shape
    weights = [w.reshape(-1, full) for w in (gate_weight, up_weight, down_weight)]
    experts = local * far * near
    rows, width = tokens.shape
    features = [(x ^ dx) * 2 + (c ^ dc) for dx in range(cols) for dc in range(2)]
    where = Cell(jnp.stack([me] + features).astype(jnp.int32))
    labels = [(dy, dx) for dy in range(near) for dx in range(cols)]
    depth = {l: bin(l[0]).count("1") + bin(l[1]).count("1") for l in labels}
    depths = max(depth.values())

    spread = jax.nn.one_hot(expert_ids, experts, dtype=jnp.float32)
    probs = jnp.sum(spread * gate_probs[:, :, None], axis=1).T
    parts = []
    for _ in range(3):
        parts.append(lax.reduce_precision(probs, 8, 7))
        probs = probs - parts[-1]
    table = jnp.concatenate(parts, axis=1).astype(jnp.bfloat16)
    table = jnp.pad(table, ((0, padded(experts) - experts), (0, width - 3 * rows)))

    have = [{} for _ in range(far)]
    have[0][0, 0, 0] = [Cell(jnp.concatenate([tokens, grad_out, table], axis=0))]

    def far_ops(q):
        return [(q, (0, 0, 0), [(c, None) for c in have[0][0, 0, 0]], "far", q)] if 0 < q < far else []

    line = far == 4
    inner = (z == 1) | (z == 2)
    outward, across = [(1, 0), (2, 3)], [(1, 2), (2, 1)]
    held = {}

    def line_sources(r):
        if r == 0:
            return [have[0][0, 0, 0][0]]
        if r == 1:
            return [held["across"], have[1][0, 0, 0][0]]
        return [held["inner"]] if r == 2 else []

    def line_step(r):
        if r == 0:
            own = have[0][0, 0, 0][0].v
            have[1][0, 0, 0] = [Cell(exchange(own, "far", 1))]
            held["across"] = Cell(passed(own, "far", across))
            return [have[1][0, 0, 0][0], held["across"]]
        if r == 1:
            held["outer"] = Cell(passed(held["across"].v, "far", outward))
            held["inner"] = Cell(passed(have[1][0, 0, 0][0].v, "far", across))
            return [held["outer"], held["inner"]]
        if r == 2:
            held["last"] = Cell(passed(held["inner"].v, "far", outward))
            return [held["last"]]
        return []

    def line_arrive(r):
        if r == 2:
            have[2][0, 0, 0] = [Cell(jnp.where(inner, held["inner"].v, held["outer"].v))]
        if r == 3:
            have[3][0, 0, 0] = [Cell(jnp.where(inner, held["across"].v, held["last"].v))]

    def level_ops(q, level):
        ops = []
        for dy, dx in labels:
            if depth[dy, dx] != level:
                continue
            if dy and dx:
                by_near, by_col = have[q][dy ^ last_bit(dy), dx, 0], have[q][dy, dx ^ last_bit(dx), 0]
                t = (by_near[0], (0, rows) if len(by_near) == 1 else None)
                g = (by_col[-1], (rows, 2 * rows) if len(by_col) == 1 else None)
                ops.append((q, (dy, dx, 0), [t], "near", last_bit(dy)))
                ops.append((q, (dy, dx, 0), [g], "col", last_bit(dx)))
            elif dy:
                whole = have[q][dy ^ last_bit(dy), dx, 0]
                ops.append((q, (dy, dx, 0), [(c, None) for c in whole], "near", last_bit(dy)))
            else:
                whole = have[q][dy, dx ^ last_bit(dx), 0]
                ops.append((q, (dy, dx, 0), [(c, None) for c in whole], "col", last_bit(dx)))
        return ops

    def half_ops(q, level):
        return [
            (q, (dy, dx, 1), [(c, None) for c in have[q][dy, dx, 0]], "half", 1)
            for dy, dx in labels
            if depth[dy, dx] == level
        ]

    def compute(q):
        pieces, at = [], {}
        for l, cells in have[q].items():
            first = len(pieces)
            pieces += [c.v for c in cells]
            at[(0,) + l] = (first, 0)
            at[(1,) + l] = (first, rows) if len(cells) == 1 else (first + 1, 0)
            at[(2,) + l] = (first, 2 * rows)
        out_at = {(dy, dx): dy * cols + dx for dy, dx in labels}
        return expert_call(where.v, pieces, weights, local, experts, rows, at, out_at, near, cols)

    class Sum:
        def __init__(self, q, keep, send):
            self.q, self.fresh = q, True
            self.cells = [Cell(keep), Cell(send)]
            self.todo = [
                [(a, s) for a in o for s in reversed(bits(near if a == "near" else cols))]
                for o in (("near", "col"), ("col", "near"))
            ]

        def begin(self):
            keep, send = (c.v for c in self.cells)
            shape = (near, cols) + keep.shape[1:]
            part = shape[2] // 2
            keep, got = keep.reshape(shape), exchange(send, "half", 1).reshape(shape)
            self.fold([keep[:, :, :part], keep[:, :, part:]], [got[:, :, :part], got[:, :, part:]])
            self.fresh = False

        def left(self):
            return len(self.todo[0])

        def fold(self, keep, got):
            self.keep, self.send = [], []
            for k, g, todo in zip(keep, got, self.todo):
                dim = 0 if todo[0][0] == "near" else 1
                (k0, k1), (g0, g1) = jnp.split(k, 2, axis=dim), jnp.split(g, 2, axis=dim)
                self.send.append(Cell(added(k1, g1)))
                self.keep.append(Cell(added(k0, g0)))

        def step(self):
            self.got = [Cell(exchange(s.v, *todo.pop(0))) for s, todo in zip(self.send, self.todo)]
            return self.got

        def refold(self):
            self.fold([c.v for c in self.keep], [c.v for c in self.got])

        def home(self):
            mine = [added(k.v, g.v)[0, 0] for k, g in zip(self.keep, self.got)]
            mine = jnp.concatenate(mine, axis=0)
            return exchange(mine, "far", self.q) if self.q else mine

    ready, sums, total = [where], [], None
    r = 0
    while r < far + depths or sums:
        if line and r:
            together(ready + line_sources(r))
            ready = ready[:1]
            line_arrive(r)
        ops = []
        for q in range(far):
            if 0 <= r - q < depths:
                ops += level_ops(q, r - q + 1)
        ops += [] if line else far_ops(r + 1)
        for q in range(far):
            if 0 <= r - q <= depths:
                ops += half_ops(q, r - q)
        if r and not line:
            together(ready + [c for o in ops for c, _ in o[2]])
        ready = ready[:1] if not r else []
        if line:
            ready += line_step(r)
        for s in list(sums):
            if not s.fresh and not s.left():
                mine = s.home().astype(jnp.float32)
                total = mine if total is None else total + mine
                sums.remove(s)
        for s in sums:
            if not s.fresh:
                s.refold()
                ready += s.step()
        for q, label, sources, axis, bit in ops:
            for c, cut in sources:
                got = Cell(exchange(c.v if cut is None else c.v[cut[0] : cut[1]], axis, bit))
                have[q].setdefault(label, []).append(got)
                if axis != "half":
                    ready.append(got)
        for s in sums:
            if s.fresh:
                s.begin()
                if 0 <= r - depths < far:
                    together(s.send + [where])
                ready += s.step()
        if 0 <= r - depths < far:
            s = Sum(r - depths, *compute(r - depths))
            sums.append(s)
            ready += s.cells
        r += 1

    grad_tokens = total[:rows].astype(jnp.bfloat16)
    by_expert = total[rows:].reshape(-1, rows)[:experts]
    grad_gates = jnp.sum(spread * by_expert.T[:, None, :], axis=2)
    return (grad_tokens, grad_gates.astype(jnp.bfloat16))


def solution(mesh):
    expert, ctx = mesh.shape["expert"], mesh.shape["ctx"]
    fine = Mesh(mesh.devices.reshape(expert // 2, 2, ctx // 2, 2), ("far", "near", "col", "half"))
    e, c = ("far", "near"), ("col", "half")
    return jax.shard_map(
        body,
        mesh=fine,
        in_specs=(P(e, c), P(e, c), P(e), P(e), P(e, c), P(e, c), P(e, c)),
        out_specs=(P(e, c), P(e)),
        check_vma=False,
    )
```

```python
import functools
import jax
import jax.numpy as jnp
from jax import lax
from jax.experimental import pallas as pl
from jax.experimental.pallas import tpu as pltpu
from jax.sharding import Mesh, PartitionSpec as P

NT = (((1,), (1,)), ((), ()))
NN = (((1,), (0,)), ((), ()))
TN = (((0,), (0,)), ((), ()))


def padded(count):
    return 16 * -(-count // 16)


def expert_kernel(plan, *refs):
    at, out_at, n_in, ndy, ndx, local, experts, rows, tile, wide = plan
    where = refs[0]
    pieces = refs[1 : 1 + n_in]
    wg, wu, wd, keep, send, d_gate, d_up, score = refs[1 + n_in :]
    width = pieces[0].shape[1]
    units = wg.shape[0]
    hidden = units // local
    blocks = [(dx, dc) for dx in range(ndx) for dc in range(2)]

    def feature(dx, dc):
        return pl.multiple_of(where[1 + 2 * dx + dc] * width, width)

    def part(kind, dy, dx, dc):
        ref, first = at[kind, dy, dx, dc]
        return pieces[ref][first : first + rows]

    def product(kind, ref, first):
        total = None
        for dx, dc in blocks:
            x = jnp.concatenate([part(kind, dy, dx, dc) for dy in range(ndy)], axis=0)
            w = ref[pl.ds(first, tile), pl.ds(feature(dx, dc), width)]
            term = lax.dot_general(x, w, NT, preferred_element_type=jnp.float32)
            total = term if total is None else total + term
        return total

    slots = padded(experts)
    expert = lax.broadcasted_iota(jnp.int32, (slots, 128), 0)
    column = lax.broadcasted_iota(jnp.int32, (slots, 128), 1)
    mine = jnp.where((expert == where[0] * local + column) & (column < local), 1.0, 0.0).astype(jnp.bfloat16)
    shares = []
    for dy in range(ndy):
        ref, first = at[2, dy, 0, 0]
        table = pieces[ref][first : first + slots]
        shares.append(
            sum(
                lax.dot_general(
                    table[:, i * rows : (i + 1) * rows], mine, TN, preferred_element_type=jnp.float32
                )
                for i in range(3)
            )
        )
    shares = jnp.concatenate(shares, axis=0)
    score[...] = jnp.zeros(score.shape, jnp.float32)

    @pl.loop(0, units // tile)
    def _(n):
        first = pl.multiple_of(n * tile, tile)
        gate, up, hid = product(0, wg, first), product(0, wu, first), product(1, wd, first)
        unit = first + lax.broadcasted_iota(jnp.int32, gate.shape, 1)
        share = jnp.zeros(gate.shape, jnp.float32)
        sig = jax.nn.sigmoid(gate)
        act = gate * sig
        both = up * hid
        scores = act * both
        for e in range(local):
            inside = (unit >= e * hidden) & (unit < (e + 1) * hidden)
            share = jnp.where(inside, shares[:, e : e + 1], share)
        row = lax.broadcasted_iota(jnp.int32, (score.shape[0], tile), 0) * hidden
        of = first + lax.broadcasted_iota(jnp.int32, (score.shape[0], tile), 1)
        pick = jnp.where((of >= row) & (of < row + hidden), 1.0, 0.0).astype(jnp.bfloat16)
        high = scores.astype(jnp.bfloat16)
        low = (scores - high.astype(jnp.float32)).astype(jnp.bfloat16)
        score[...] += lax.dot_general(pick, high, NT, preferred_element_type=jnp.float32) + lax.dot_general(
            pick, low, NT, preferred_element_type=jnp.float32
        )
        d_gate[:, pl.ds(first, tile)] = (share * (both * sig * (1.0 + gate * (1.0 - sig)))).astype(
            jnp.bfloat16
        )
        d_up[:, pl.ds(first, tile)] = (share * (hid * act)).astype(jnp.bfloat16)

    extra = keep.shape[1] - rows
    per_row = width // rows
    place = lax.broadcasted_iota(jnp.int32, (extra, width), 0) * per_row
    place = place + lax.broadcasted_iota(jnp.int32, (extra, width), 1) // rows
    for dy in range(ndy):
        table = jnp.zeros((extra, width), jnp.float32)
        for e in range(local):
            line = jnp.concatenate([score[e : e + 1, dy * rows : (dy + 1) * rows]] * per_row, axis=1)
            table = jnp.where(place == where[0] * local + e, line, table)
        for dx, dc in blocks:
            (keep, send)[dc][out_at[dy, dx], rows:, :] = table.astype(jnp.bfloat16)

    for dx, dc in blocks:

        @pl.loop(0, width // wide)
        def _(n):
            start = pl.multiple_of(n * wide, wide)
            source = pl.ds(pl.multiple_of(feature(dx, dc) + start, wide), wide)
            total = lax.dot_general(
                d_gate[...], wg[:, source], NN, preferred_element_type=jnp.float32
            ) + lax.dot_general(d_up[...], wu[:, source], NN, preferred_element_type=jnp.float32)
            total = total.astype(jnp.bfloat16)
            for dy in range(ndy):
                (keep, send)[dc][out_at[dy, dx], :rows, pl.ds(start, wide)] = total[dy * rows : (dy + 1) * rows]


def expert_call(where, pieces, weights, local, experts, rows, at, out_at, ndy, ndx):
    units, full = weights[0].shape
    width = pieces[0].shape[1]
    tile = next(t for t in (256, 128, 64, 32, 16) if units % t == 0)
    wide = next(t for t in (1024, 512, 256, 128) if width % t == 0)
    vmem = pl.BlockSpec(memory_space=pltpu.VMEM)
    extra = padded(-(-experts // (width // rows)))
    out = jax.ShapeDtypeStruct((ndy * ndx, rows + extra, width), jnp.bfloat16)
    m = ndy * rows
    return pl.pallas_call(
        functools.partial(
            expert_kernel, (at, out_at, len(pieces), ndy, ndx, local, experts, rows, tile, wide)
        ),
        in_specs=[pl.BlockSpec(memory_space=pltpu.SMEM)] + [vmem] * (len(pieces) + 3),
        out_specs=[vmem] * 2,
        scratch_shapes=[pltpu.VMEM((m, units), jnp.bfloat16)] * 2
        + [pltpu.VMEM((padded(local), m), jnp.float32)],
        out_shape=[out] * 2,
        compiler_params=pltpu.CompilerParams(vmem_limit_bytes=16 << 20),
        cost_estimate=pl.CostEstimate(
            flops=10 * m * units * full, bytes_accessed=6 * units * full, transcendentals=0
        ),
    )(where, *pieces, *weights)


def exchange(x, axis, step):
    return lax.ppermute(x, axis, [(i, i ^ step) for i in range(lax.axis_size(axis))])


def passed(x, axis, pairs):
    return lax.ppermute(x, axis, pairs)


def bits(size):
    return [1 << b for b in range(size.bit_length() - 1)]


def last_bit(v):
    return 1 << (v.bit_length() - 1)


def added(a, b):
    return (a.astype(jnp.float32) + b.astype(jnp.float32)).astype(jnp.bfloat16)


class Cell:
    def __init__(self, value):
        self.v = value


def together(cells):
    cells = list({id(c): c for c in cells}.values())
    if len(cells) > 1:
        for c, v in zip(cells, lax.optimization_barrier([c.v for c in cells])):
            c.v = v


def exchange(x, axis, step):
    return lax.ppermute(x, axis, [(i, i ^ step) for i in range(lax.axis_size(axis))])


def passed(x, axis, pairs):
    return lax.ppermute(x, axis, pairs)


def bits(size):
    return [1 << b for b in range(size.bit_length() - 1)]


def last_bit(v):
    return 1 << (v.bit_length() - 1)


def added(a, b):
    return (a.astype(jnp.float32) + b.astype(jnp.float32)).astype(jnp.bfloat16)


class Cell:
    def __init__(self, value):
        self.v = value


def together(cells):
    cells = list({id(c): c for c in cells}.values())
    if len(cells) > 1:
        for c, v in zip(cells, lax.optimization_barrier([c.v for c in cells])):
            c.v = v


def touch_kernel(where, *refs):
    for i in range(where.shape[0]):
        refs[-1][i] = where[i]


def touch_call(where, arrays):
    smem, vmem = pl.BlockSpec(memory_space=pltpu.SMEM), pl.BlockSpec(memory_space=pltpu.VMEM)
    return pl.pallas_call(
        touch_kernel,
        in_specs=[smem] + [vmem] * len(arrays),
        out_specs=smem,
        out_shape=jax.ShapeDtypeStruct(where.shape, where.dtype),
        compiler_params=pltpu.CompilerParams(vmem_limit_bytes=2 << 20),
    )(where, *arrays)


def body(tokens, grad_out, expert_ids, gate_probs, gate_weight, up_weight, down_weight):
    far, near, cols = lax.axis_size("far"), lax.axis_size("near"), lax.axis_size("col")
    z, y, x, c = (lax.axis_index(n) for n in ("far", "near", "col", "half"))
    me = z * near + y
    local, _, full = gate_weight.shape
    weights = [w.reshape(-1, full) for w in (gate_weight, up_weight, down_weight)]
    experts = local * far * near
    rows, width = tokens.shape
    features = [(x ^ dx) * 2 + (c ^ dc) for dx in range(cols) for dc in range(2)]
    where = Cell(jnp.stack([me] + features).astype(jnp.int32))
    labels = [(dy, dx) for dy in range(near) for dx in range(cols)]
    depth = {l: bin(l[0]).count("1") + bin(l[1]).count("1") for l in labels}
    depths = max(depth.values())

    spread = jax.nn.one_hot(expert_ids, experts, dtype=jnp.float32)
    probs = jnp.sum(spread * gate_probs[:, :, None], axis=1).T
    parts = []
    for _ in range(3):
        parts.append(lax.reduce_precision(probs, 8, 7))
        probs = probs - parts[-1]
    table = jnp.concatenate(parts, axis=1).astype(jnp.bfloat16)
    table = jnp.pad(table, ((0, padded(experts) - experts), (0, width - 3 * rows)))

    have = [{} for _ in range(far)]
    have[0][0, 0, 0] = [Cell(jnp.concatenate([tokens, grad_out, table], axis=0))]

    def far_ops(q):
        return [(q, (0, 0, 0), [(c, None) for c in have[0][0, 0, 0]], "far", q)] if 0 < q < far else []

    line = far == 4
    inner = (z == 1) | (z == 2)
    outward, across = [(1, 0), (2, 3)], [(1, 2), (2, 1)]
    held = {}

    def line_sources(r):
        if r == 0:
            return [have[0][0, 0, 0][0]]
        if r == 1:
            return [held["across"], have[1][0, 0, 0][0]]
        return [held["inner"]] if r == 2 else []

    def line_step(r):
        if r == 0:
            own = have[0][0, 0, 0][0].v
            have[1][0, 0, 0] = [Cell(exchange(own, "far", 1))]
            held["across"] = Cell(passed(own, "far", across))
            return [have[1][0, 0, 0][0], held["across"]]
        if r == 1:
            held["outer"] = Cell(passed(held["across"].v, "far", outward))
            held["inner"] = Cell(passed(have[1][0, 0, 0][0].v, "far", across))
            return [held["outer"], held["inner"]]
        if r == 2:
            held["last"] = Cell(passed(held["inner"].v, "far", outward))
            return [held["last"]]
        return []

    def line_arrive(r):
        if r == 2:
            have[2][0, 0, 0] = [Cell(jnp.where(inner, held["inner"].v, held["outer"].v))]
        if r == 3:
            have[3][0, 0, 0] = [Cell(jnp.where(inner, held["across"].v, held["last"].v))]

    def level_ops(q, level):
        ops = []
        for dy, dx in labels:
            if depth[dy, dx] != level:
                continue
            if dy and dx and q % 2:
                whole = have[q][dy, dx ^ last_bit(dx), 0]
                ops.append((q, (dy, dx, 0), [(c, None) for c in whole], "col", last_bit(dx)))
            elif dy and dx:
                by_near, by_col = have[q][dy ^ last_bit(dy), dx, 0], have[q][dy, dx ^ last_bit(dx), 0]
                t = (by_near[0], (0, rows) if len(by_near) == 1 else None)
                g = (by_col[-1], (rows, 2 * rows) if len(by_col) == 1 else None)
                ops.append((q, (dy, dx, 0), [t], "near", last_bit(dy)))
                ops.append((q, (dy, dx, 0), [g], "col", last_bit(dx)))
            elif dy:
                whole = have[q][dy ^ last_bit(dy), dx, 0]
                ops.append((q, (dy, dx, 0), [(c, None) for c in whole], "near", last_bit(dy)))
            else:
                whole = have[q][dy, dx ^ last_bit(dx), 0]
                ops.append((q, (dy, dx, 0), [(c, None) for c in whole], "col", last_bit(dx)))
        return ops

    def half_ops(q, level):
        return [
            (q, (dy, dx, 1), [(c, None) for c in have[q][dy, dx, 0]], "half", 1)
            for dy, dx in labels
            if depth[dy, dx] == level
        ]

    def compute(q):
        pieces, at = [], {}
        for l, cells in have[q].items():
            first = len(pieces)
            pieces += [c.v for c in cells]
            at[(0,) + l] = (first, 0)
            at[(1,) + l] = (first, rows) if len(cells) == 1 else (first + 1, 0)
            at[(2,) + l] = (first, 2 * rows)
        out_at = {(dy, dx): dy * cols + dx for dy, dx in labels}
        return expert_call(where, pieces, weights, local, experts, rows, at, out_at, near, cols)

    class Sum:
        def __init__(self, q, keep, send):
            self.q, self.half, self.todo, self.mine = q, None, None, None
            self.cells = [Cell(keep), Cell(send)]
            self.urgent = q > 0
            self.orders = [("near", "col"), ("col", "near")][: 2 if self.urgent else 1]

        def begin(self):
            self.half = Cell(exchange(self.cells[1].v, "half", 1))

        def first(self):
            keep = self.cells[0].v
            shape = (near, cols) + keep.shape[1:]
            part = shape[2] // len(self.orders)
            keep, got = keep.reshape(shape), self.half.v.reshape(shape)
            cut = lambda x: [x[:, :, i * part : (i + 1) * part] for i in range(len(self.orders))]
            self.todo = [
                [(a, s) for a in o for s in reversed(bits(near if a == "near" else cols))] for o in self.orders
            ]
            self.fold(cut(keep), cut(got))

        def left(self):
            return len(self.todo[0])

        def fold(self, keep, got):
            self.keep, self.send = [], []
            for k, g, todo in zip(keep, got, self.todo):
                dim = 0 if todo[0][0] == "near" else 1
                (k0, k1), (g0, g1) = jnp.split(k, 2, axis=dim), jnp.split(g, 2, axis=dim)
                self.send.append(Cell(added(k1, g1)))
                self.keep.append(Cell(added(k0, g0)))

        def step(self):
            self.got = [Cell(exchange(s.v, *todo.pop(0))) for s, todo in zip(self.send, self.todo)]
            return self.got

        def refold(self):
            self.fold([c.v for c in self.keep], [c.v for c in self.got])

        def finish(self):
            mine = [added(k.v, g.v)[0, 0] for k, g in zip(self.keep, self.got)]
            self.mine = Cell(mine[0] if len(mine) == 1 else jnp.concatenate(mine, axis=0))

        def home(self):
            homes.append(Cell(exchange(self.mine.v, "far", self.q) if self.q else self.mine.v))
            sums.remove(self)

    where = where.v
    ready, sums, homes, held_back = [], [], [], []
    r = 0
    while r < far + depths or sums:
        if line and r:
            together(ready + line_sources(r))
            line_arrive(r)
        ops = []
        for q in range(far):
            if 0 <= r - q < depths:
                ops += level_ops(q, r - q + 1)
        ops += [] if line else far_ops(r + 1)
        for q in range(far):
            if 0 <= r - q <= depths:
                ops += half_ops(q, r - q)
        if r and not line:
            together(ready + [c for o in ops for c, _ in o[2]])
        ready = line_step(r) if line else []
        working = r - depths if 0 <= r - depths < far else None
        begun = []
        for s in list(sums):
            if s.half is None:
                s.begin()
                if s.urgent:
                    s.first()
                    begun.append(s)
                else:
                    ready.append(s.half)
            elif s.todo is None:
                s.first()
                ready += s.step()
            elif s.left():
                s.refold()
                ready += s.step()
            elif s.mine is None:
                s.finish()
                s.home()
        for q, label, sources, axis, bit in ops:
            for c, cut in sources:
                got = Cell(exchange(c.v if cut is None else c.v[cut[0] : cut[1]], axis, bit))
                have[q].setdefault(label, []).append(got)
                if axis != "half":
                    ready.append(got)
        if begun and working is not None:
            together([c for s in begun for c in s.send] + have[working][0, 0, 0])
        for s in begun:
            ready += s.step()
        ready, held_back = ready + held_back, []
        if begun and working is None:
            for s in [s for s in sums if s.q == far - 2 and not s.left()]:
                s.finish()
                s.home()
                held_back.append(homes[-1])
        if working is not None:
            s = Sum(working, *compute(working))
            sums.append(s)
            ready += s.cells
        r += 1
    total = sum(h.v.astype(jnp.float32) for h in homes)

    grad_tokens = total[:rows].astype(jnp.bfloat16)
    by_expert = total[rows:].reshape(-1, rows)[:experts]
    grad_gates = jnp.sum(spread * by_expert.T[:, None, :], axis=2)
    return (grad_tokens, grad_gates.astype(jnp.bfloat16))


def solution(mesh):
    expert, ctx = mesh.shape["expert"], mesh.shape["ctx"]
    fine = Mesh(mesh.devices.reshape(expert // 2, 2, ctx // 2, 2), ("far", "near", "col", "half"))
    e, c = ("far", "near"), ("col", "half")
    return jax.shard_map(
        body,
        mesh=fine,
        in_specs=(P(e, c), P(e, c), P(e), P(e), P(e, c), P(e, c), P(e, c)),
        out_specs=(P(e, c), P(e)),
        check_vma=False,
    )
```

```python
import functools
import jax
import jax.numpy as jnp
from jax import lax
from jax.experimental import pallas as pl
from jax.experimental.pallas import tpu as pltpu
from jax.sharding import Mesh, PartitionSpec as P

NT = (((1,), (1,)), ((), ()))
NN = (((1,), (0,)), ((), ()))
TN = (((0,), (0,)), ((), ()))


def padded(count):
    return 16 * -(-count // 16)


def expert_kernel(plan, *refs):
    at, out_at, n_in, ndy, ndx, local, experts, rows, tile, wide = plan
    where = refs[0]
    pieces = refs[1 : 1 + n_in]
    wg, wu, wd, keep, send, d_gate, d_up, score = refs[1 + n_in :]
    width = pieces[0].shape[1]
    units = wg.shape[0]
    hidden = units // local
    blocks = [(dx, dc) for dx in range(ndx) for dc in range(2)]

    def feature(dx, dc):
        return pl.multiple_of(where[1 + 2 * dx + dc] * width, width)

    def part(kind, dy, dx, dc):
        ref, first = at[kind, dy, dx, dc]
        return pieces[ref][first : first + rows]

    def product(kind, ref, first):
        total = None
        for dx, dc in blocks:
            x = jnp.concatenate([part(kind, dy, dx, dc) for dy in range(ndy)], axis=0)
            w = ref[pl.ds(first, tile), pl.ds(feature(dx, dc), width)]
            term = lax.dot_general(x, w, NT, preferred_element_type=jnp.float32)
            total = term if total is None else total + term
        return total

    slots = padded(experts)
    expert = lax.broadcasted_iota(jnp.int32, (slots, 128), 0)
    column = lax.broadcasted_iota(jnp.int32, (slots, 128), 1)
    mine = jnp.where((expert == where[0] * local + column) & (column < local), 1.0, 0.0).astype(jnp.bfloat16)
    shares = []
    for dy in range(ndy):
        ref, first = at[2, dy, 0, 0]
        table = pieces[ref][first : first + slots]
        shares.append(
            sum(
                lax.dot_general(
                    table[:, i * rows : (i + 1) * rows], mine, TN, preferred_element_type=jnp.float32
                )
                for i in range(3)
            )
        )
    shares = jnp.concatenate(shares, axis=0)
    score[...] = jnp.zeros(score.shape, jnp.float32)

    @pl.loop(0, units // tile)
    def _(n):
        first = pl.multiple_of(n * tile, tile)
        gate, up, hid = product(0, wg, first), product(0, wu, first), product(1, wd, first)
        unit = first + lax.broadcasted_iota(jnp.int32, gate.shape, 1)
        share = jnp.zeros(gate.shape, jnp.float32)
        sig = jax.nn.sigmoid(gate)
        act = gate * sig
        both = up * hid
        scores = act * both
        for e in range(local):
            inside = (unit >= e * hidden) & (unit < (e + 1) * hidden)
            share = jnp.where(inside, shares[:, e : e + 1], share)
        row = lax.broadcasted_iota(jnp.int32, (score.shape[0], tile), 0) * hidden
        of = first + lax.broadcasted_iota(jnp.int32, (score.shape[0], tile), 1)
        pick = jnp.where((of >= row) & (of < row + hidden), 1.0, 0.0).astype(jnp.bfloat16)
        high = scores.astype(jnp.bfloat16)
        low = (scores - high.astype(jnp.float32)).astype(jnp.bfloat16)
        score[...] += lax.dot_general(pick, high, NT, preferred_element_type=jnp.float32) + lax.dot_general(
            pick, low, NT, preferred_element_type=jnp.float32
        )
        d_gate[:, pl.ds(first, tile)] = (share * (both * sig * (1.0 + gate * (1.0 - sig)))).astype(
            jnp.bfloat16
        )
        d_up[:, pl.ds(first, tile)] = (share * (hid * act)).astype(jnp.bfloat16)

    extra = keep.shape[1] - rows
    per_row = width // rows
    place = lax.broadcasted_iota(jnp.int32, (extra, width), 0) * per_row
    place = place + lax.broadcasted_iota(jnp.int32, (extra, width), 1) // rows
    for dy in range(ndy):
        table = jnp.zeros((extra, width), jnp.float32)
        for e in range(local):
            line = jnp.concatenate([score[e : e + 1, dy * rows : (dy + 1) * rows]] * per_row, axis=1)
            table = jnp.where(place == where[0] * local + e, line, table)
        for dx, dc in blocks:
            (keep, send)[dc][out_at[dy, dx], rows:, :] = table.astype(jnp.bfloat16)

    for dx, dc in blocks:

        @pl.loop(0, width // wide)
        def _(n):
            start = pl.multiple_of(n * wide, wide)
            source = pl.ds(pl.multiple_of(feature(dx, dc) + start, wide), wide)
            total = lax.dot_general(
                d_gate[...], wg[:, source], NN, preferred_element_type=jnp.float32
            ) + lax.dot_general(d_up[...], wu[:, source], NN, preferred_element_type=jnp.float32)
            total = total.astype(jnp.bfloat16)
            for dy in range(ndy):
                (keep, send)[dc][out_at[dy, dx], :rows, pl.ds(start, wide)] = total[dy * rows : (dy + 1) * rows]


def expert_call(where, pieces, weights, local, experts, rows, at, out_at, ndy, ndx):
    units, full = weights[0].shape
    width = pieces[0].shape[1]
    tile = next(t for t in (256, 128, 64, 32, 16) if units % t == 0)
    wide = next(t for t in (1024, 512, 256, 128) if width % t == 0)
    vmem = pl.BlockSpec(memory_space=pltpu.VMEM)
    extra = padded(-(-experts // (width // rows)))
    out = jax.ShapeDtypeStruct((ndy * ndx, rows + extra, width), jnp.bfloat16)
    m = ndy * rows
    return pl.pallas_call(
        functools.partial(
            expert_kernel, (at, out_at, len(pieces), ndy, ndx, local, experts, rows, tile, wide)
        ),
        in_specs=[pl.BlockSpec(memory_space=pltpu.SMEM)] + [vmem] * (len(pieces) + 3),
        out_specs=[vmem] * 2,
        scratch_shapes=[pltpu.VMEM((m, units), jnp.bfloat16)] * 2
        + [pltpu.VMEM((padded(local), m), jnp.float32)],
        out_shape=[out] * 2,
        compiler_params=pltpu.CompilerParams(vmem_limit_bytes=16 << 20),
        cost_estimate=pl.CostEstimate(
            flops=10 * m * units * full, bytes_accessed=6 * units * full, transcendentals=0
        ),
    )(where, *pieces, *weights)


def exchange(x, axis, step):
    return lax.ppermute(x, axis, [(i, i ^ step) for i in range(lax.axis_size(axis))])


def passed(x, axis, pairs):
    return lax.ppermute(x, axis, pairs)


def bits(size):
    return [1 << b for b in range(size.bit_length() - 1)]


def last_bit(v):
    return 1 << (v.bit_length() - 1)


def added(a, b):
    return (a.astype(jnp.float32) + b.astype(jnp.float32)).astype(jnp.bfloat16)


class Cell:
    def __init__(self, value):
        self.v = value


def together(cells):
    cells = list({id(c): c for c in cells}.values())
    if len(cells) > 1:
        for c, v in zip(cells, lax.optimization_barrier([c.v for c in cells])):
            c.v = v


def exchange(x, axis, step):
    return lax.ppermute(x, axis, [(i, i ^ step) for i in range(lax.axis_size(axis))])


def passed(x, axis, pairs):
    return lax.ppermute(x, axis, pairs)


def bits(size):
    return [1 << b for b in range(size.bit_length() - 1)]


def last_bit(v):
    return 1 << (v.bit_length() - 1)


def added(a, b):
    return (a.astype(jnp.float32) + b.astype(jnp.float32)).astype(jnp.bfloat16)


class Cell:
    def __init__(self, value):
        self.v = value


def together(cells):
    cells = list({id(c): c for c in cells}.values())
    if len(cells) > 1:
        for c, v in zip(cells, lax.optimization_barrier([c.v for c in cells])):
            c.v = v


def touch_kernel(where, *refs):
    for i in range(where.shape[0]):
        refs[-1][i] = where[i]


def touch_call(where, arrays):
    smem, vmem = pl.BlockSpec(memory_space=pltpu.SMEM), pl.BlockSpec(memory_space=pltpu.VMEM)
    return pl.pallas_call(
        touch_kernel,
        in_specs=[smem] + [vmem] * len(arrays),
        out_specs=smem,
        out_shape=jax.ShapeDtypeStruct(where.shape, where.dtype),
        compiler_params=pltpu.CompilerParams(vmem_limit_bytes=2 << 20),
    )(where, *arrays)


def body(tokens, grad_out, expert_ids, gate_probs, gate_weight, up_weight, down_weight):
    far, near, cols = lax.axis_size("far"), lax.axis_size("near"), lax.axis_size("col")
    z, y, x, c = (lax.axis_index(n) for n in ("far", "near", "col", "half"))
    me = z * near + y
    local, _, full = gate_weight.shape
    weights = [w.reshape(-1, full) for w in (gate_weight, up_weight, down_weight)]
    experts = local * far * near
    rows, width = tokens.shape
    features = [(x ^ dx) * 2 + (c ^ dc) for dx in range(cols) for dc in range(2)]
    where = Cell(jnp.stack([me] + features).astype(jnp.int32))
    labels = [(dy, dx) for dy in range(near) for dx in range(cols)]
    depth = {l: bin(l[0]).count("1") + bin(l[1]).count("1") for l in labels}
    depths = max(depth.values())

    spread = jax.nn.one_hot(expert_ids, experts, dtype=jnp.float32)
    probs = jnp.sum(spread * gate_probs[:, :, None], axis=1).T
    parts = []
    for _ in range(3):
        parts.append(lax.reduce_precision(probs, 8, 7))
        probs = probs - parts[-1]
    table = jnp.concatenate(parts, axis=1).astype(jnp.bfloat16)
    table = jnp.pad(table, ((0, padded(experts) - experts), (0, width - 3 * rows)))

    have = [{} for _ in range(far)]
    have[0][0, 0, 0] = [Cell(jnp.concatenate([tokens, grad_out, table], axis=0))]

    def far_ops(q):
        return [(q, (0, 0, 0), [(c, None) for c in have[0][0, 0, 0]], "far", q)] if 0 < q < far else []

    line = far == 4
    inner = (z == 1) | (z == 2)
    outward, across = [(1, 0), (2, 3)], [(1, 2), (2, 1)]
    held = {}

    def line_sources(r):
        if r == 0:
            return [have[0][0, 0, 0][0]]
        if r == 1:
            return [held["across"], have[1][0, 0, 0][0]]
        return [held["inner"]] if r == 2 else []

    def line_step(r):
        if r == 0:
            own = have[0][0, 0, 0][0].v
            have[1][0, 0, 0] = [Cell(exchange(own, "far", 1))]
            held["across"] = Cell(passed(own, "far", across))
            return [have[1][0, 0, 0][0], held["across"]]
        if r == 1:
            held["outer"] = Cell(passed(held["across"].v, "far", outward))
            held["inner"] = Cell(passed(have[1][0, 0, 0][0].v, "far", across))
            return [held["outer"], held["inner"]]
        if r == 2:
            held["last"] = Cell(passed(held["inner"].v, "far", outward))
            return [held["last"]]
        return []

    def line_arrive(r):
        if r == 2:
            have[2][0, 0, 0] = [Cell(jnp.where(inner, held["inner"].v, held["outer"].v))]
        if r == 3:
            have[3][0, 0, 0] = [Cell(jnp.where(inner, held["across"].v, held["last"].v))]

    def level_ops(q, level):
        ops = []
        for dy, dx in labels:
            if depth[dy, dx] != level:
                continue
            if dy and dx and q % 4 not in (0,2,3,):
                whole = have[q][dy, dx ^ last_bit(dx), 0]
                ops.append((q, (dy, dx, 0), [(c, None) for c in whole], "col", last_bit(dx)))
            elif dy and dx:
                by_near, by_col = have[q][dy ^ last_bit(dy), dx, 0], have[q][dy, dx ^ last_bit(dx), 0]
                t = (by_near[0], (0, rows) if len(by_near) == 1 else None)
                g = (by_col[-1], (rows, 2 * rows) if len(by_col) == 1 else None)
                ops.append((q, (dy, dx, 0), [t], "near", last_bit(dy)))
                ops.append((q, (dy, dx, 0), [g], "col", last_bit(dx)))
            elif dy:
                whole = have[q][dy ^ last_bit(dy), dx, 0]
                ops.append((q, (dy, dx, 0), [(c, None) for c in whole], "near", last_bit(dy)))
            else:
                whole = have[q][dy, dx ^ last_bit(dx), 0]
                ops.append((q, (dy, dx, 0), [(c, None) for c in whole], "col", last_bit(dx)))
        return ops

    def half_ops(q, level):
        return [
            (q, (dy, dx, 1), [(c, None) for c in have[q][dy, dx, 0]], "half", 1)
            for dy, dx in labels
            if depth[dy, dx] == level
        ]

    def compute(q):
        pieces, at = [], {}
        for l, cells in have[q].items():
            first = len(pieces)
            pieces += [c.v for c in cells]
            at[(0,) + l] = (first, 0)
            at[(1,) + l] = (first, rows) if len(cells) == 1 else (first + 1, 0)
            at[(2,) + l] = (first, 2 * rows)
        out_at = {(dy, dx): dy * cols + dx for dy, dx in labels}
        return expert_call(where, pieces, weights, local, experts, rows, at, out_at, near, cols)

    class Sum:
        def __init__(self, q, keep, send):
            self.q, self.half, self.todo, self.mine = q, None, None, None
            self.cells = [Cell(keep), Cell(send)]
            self.urgent = q > 0
            self.orders = [("near", "col"), ("col", "near")]

        def begin(self):
            self.half = Cell(exchange(self.cells[1].v, "half", 1))

        def first(self):
            keep = self.cells[0].v
            shape = (near, cols) + keep.shape[1:]
            part = shape[2] // len(self.orders)
            keep, got = keep.reshape(shape), self.half.v.reshape(shape)
            cut = lambda x: [x[:, :, i * part : (i + 1) * part] for i in range(len(self.orders))]
            self.todo = [
                [(a, s) for a in o for s in reversed(bits(near if a == "near" else cols))] for o in self.orders
            ]
            self.fold(cut(keep), cut(got))

        def left(self):
            return len(self.todo[0])

        def fold(self, keep, got):
            self.keep, self.send = [], []
            for k, g, todo in zip(keep, got, self.todo):
                dim = 0 if todo[0][0] == "near" else 1
                (k0, k1), (g0, g1) = jnp.split(k, 2, axis=dim), jnp.split(g, 2, axis=dim)
                self.send.append(Cell(added(k1, g1)))
                self.keep.append(Cell(added(k0, g0)))

        def step(self):
            self.got = [Cell(exchange(s.v, *todo.pop(0))) for s, todo in zip(self.send, self.todo)]
            return self.got

        def refold(self):
            self.fold([c.v for c in self.keep], [c.v for c in self.got])

        def finish(self):
            mine = [added(k.v, g.v)[0, 0] for k, g in zip(self.keep, self.got)]
            self.mine = Cell(mine[0] if len(mine) == 1 else jnp.concatenate(mine, axis=0))

        def home(self):
            homes.append(Cell(exchange(self.mine.v, "far", self.q) if self.q else self.mine.v))
            sums.remove(self)

    where = where.v
    ready, sums, homes, held_back = [], [], [], []
    r = 0
    while r < far + depths or sums:
        if line and r:
            together(ready + line_sources(r))
            line_arrive(r)
        ops = []
        for q in range(far):
            if 0 <= r - q < depths:
                ops += level_ops(q, r - q + 1)
        ops += [] if line else far_ops(r + 1)
        for q in range(far):
            if 0 <= r - q <= depths:
                ops += half_ops(q, r - q)
        if r and not line:
            together(ready + [c for o in ops for c, _ in o[2]])
        ready = line_step(r) if line else []
        working = r - depths if 0 <= r - depths < far else None
        begun = []
        for s in list(sums):
            if s.half is None:
                s.begin()
                if s.urgent:
                    s.first()
                    begun.append(s)
                else:
                    ready.append(s.half)
            elif s.todo is None:
                if r >= depths + 3:
                    s.first()
                    ready += s.step()
                else:
                    ready.append(s.half)
            elif s.left() == 1 and not s.urgent and any(o.urgent and (o.todo is None or o.left()) for o in sums):
                ready += s.got
            elif s.left():
                s.refold()
                ready += s.step()
            elif s.mine is None:
                s.finish()
                s.home()
        for q, label, sources, axis, bit in ops:
            for c, cut in sources:
                got = Cell(exchange(c.v if cut is None else c.v[cut[0] : cut[1]], axis, bit))
                have[q].setdefault(label, []).append(got)
                if axis != "half":
                    ready.append(got)
        if begun and working is not None:
            together([c for s in begun for c in s.send] + have[working][0, 0, 0])
        for s in begun:
            ready += s.step()
        ready, held_back = ready + held_back, []
        if begun and working is None:
            for s in [s for s in sums if s.q == far - 2 and not s.left()]:
                s.finish()
                s.home()
                held_back.append(homes[-1])
        if working is not None:
            s = Sum(working, *compute(working))
            sums.append(s)
            ready += s.cells
        r += 1
    total = sum(h.v.astype(jnp.float32) for h in homes)

    grad_tokens = total[:rows].astype(jnp.bfloat16)
    by_expert = total[rows:].reshape(-1, rows)[:experts]
    grad_gates = jnp.sum(spread * by_expert.T[:, None, :], axis=2)
    return (grad_tokens, grad_gates.astype(jnp.bfloat16))


def solution(mesh):
    expert, ctx = mesh.shape["expert"], mesh.shape["ctx"]
    fine = Mesh(mesh.devices.reshape(expert // 2, 2, ctx // 2, 2), ("far", "near", "col", "half"))
    e, c = ("far", "near"), ("col", "half")
    return jax.shard_map(
        body,
        mesh=fine,
        in_specs=(P(e, c), P(e, c), P(e), P(e), P(e, c), P(e, c), P(e, c)),
        out_specs=(P(e, c), P(e)),
        check_vma=False,
    )
```

```python
import functools
import jax
import jax.numpy as jnp
from jax import lax
from jax.experimental import pallas as pl
from jax.experimental.pallas import tpu as pltpu
from jax.sharding import Mesh, PartitionSpec as P

NT = (((1,), (1,)), ((), ()))
NN = (((1,), (0,)), ((), ()))
TN = (((0,), (0,)), ((), ()))


def padded(count):
    return 16 * -(-count // 16)


def expert_kernel(plan, *refs):
    at, out_at, n_in, ndy, ndx, local, experts, rows, tile, wide = plan
    where = refs[0]
    pieces = refs[1 : 1 + n_in]
    wg, wu, wd, keep, send, d_gate, d_up, score = refs[1 + n_in :]
    width = pieces[0].shape[1]
    units = wg.shape[0]
    hidden = units // local
    blocks = [(dx, dc) for dx in range(ndx) for dc in range(2)]

    def feature(dx, dc):
        return pl.multiple_of(where[1 + 2 * dx + dc] * width, width)

    def part(kind, dy, dx, dc):
        ref, first = at[kind, dy, dx, dc]
        return pieces[ref][first : first + rows]

    def product(kind, ref, first):
        total = None
        for dx, dc in blocks:
            x = jnp.concatenate([part(kind, dy, dx, dc) for dy in range(ndy)], axis=0)
            w = ref[pl.ds(first, tile), pl.ds(feature(dx, dc), width)]
            term = lax.dot_general(x, w, NT, preferred_element_type=jnp.float32)
            total = term if total is None else total + term
        return total

    slots = padded(experts)
    expert = lax.broadcasted_iota(jnp.int32, (slots, 128), 0)
    column = lax.broadcasted_iota(jnp.int32, (slots, 128), 1)
    mine = jnp.where((expert == where[0] * local + column) & (column < local), 1.0, 0.0).astype(jnp.bfloat16)
    shares = []
    for dy in range(ndy):
        ref, first = at[2, dy, 0, 0]
        table = pieces[ref][first : first + slots]
        shares.append(
            sum(
                lax.dot_general(
                    table[:, i * rows : (i + 1) * rows], mine, TN, preferred_element_type=jnp.float32
                )
                for i in range(3)
            )
        )
    shares = jnp.concatenate(shares, axis=0)
    score[...] = jnp.zeros(score.shape, jnp.float32)

    @pl.loop(0, units // tile)
    def _(n):
        first = pl.multiple_of(n * tile, tile)
        gate, up, hid = product(0, wg, first), product(0, wu, first), product(1, wd, first)
        unit = first + lax.broadcasted_iota(jnp.int32, gate.shape, 1)
        share = jnp.zeros(gate.shape, jnp.float32)
        sig = jax.nn.sigmoid(gate)
        act = gate * sig
        both = up * hid
        scores = act * both
        for e in range(local):
            inside = (unit >= e * hidden) & (unit < (e + 1) * hidden)
            share = jnp.where(inside, shares[:, e : e + 1], share)
        row = lax.broadcasted_iota(jnp.int32, (score.shape[0], tile), 0) * hidden
        of = first + lax.broadcasted_iota(jnp.int32, (score.shape[0], tile), 1)
        pick = jnp.where((of >= row) & (of < row + hidden), 1.0, 0.0).astype(jnp.bfloat16)
        high = scores.astype(jnp.bfloat16)
        low = (scores - high.astype(jnp.float32)).astype(jnp.bfloat16)
        score[...] += lax.dot_general(pick, high, NT, preferred_element_type=jnp.float32) + lax.dot_general(
            pick, low, NT, preferred_element_type=jnp.float32
        )
        d_gate[:, pl.ds(first, tile)] = (share * (both * sig * (1.0 + gate * (1.0 - sig)))).astype(
            jnp.bfloat16
        )
        d_up[:, pl.ds(first, tile)] = (share * (hid * act)).astype(jnp.bfloat16)

    extra = keep.shape[1] - rows
    per_row = width // rows
    place = lax.broadcasted_iota(jnp.int32, (extra, width), 0) * per_row
    place = place + lax.broadcasted_iota(jnp.int32, (extra, width), 1) // rows
    for dy in range(ndy):
        table = jnp.zeros((extra, width), jnp.float32)
        for e in range(local):
            line = jnp.concatenate([score[e : e + 1, dy * rows : (dy + 1) * rows]] * per_row, axis=1)
            table = jnp.where(place == where[0] * local + e, line, table)
        for dx, dc in blocks:
            (keep, send)[dc][out_at[dy, dx], rows:, :] = table.astype(jnp.bfloat16)

    for dx, dc in blocks:

        @pl.loop(0, width // wide)
        def _(n):
            start = pl.multiple_of(n * wide, wide)
            source = pl.ds(pl.multiple_of(feature(dx, dc) + start, wide), wide)
            total = lax.dot_general(
                d_gate[...], wg[:, source], NN, preferred_element_type=jnp.float32
            ) + lax.dot_general(d_up[...], wu[:, source], NN, preferred_element_type=jnp.float32)
            total = total.astype(jnp.bfloat16)
            for dy in range(ndy):
                (keep, send)[dc][out_at[dy, dx], :rows, pl.ds(start, wide)] = total[dy * rows : (dy + 1) * rows]


def expert_call(where, pieces, weights, local, experts, rows, at, out_at, ndy, ndx):
    units, full = weights[0].shape
    width = pieces[0].shape[1]
    tile = next(t for t in (256, 128, 64, 32, 16) if units % t == 0)
    wide = next(t for t in (1024, 512, 256, 128) if width % t == 0)
    vmem = pl.BlockSpec(memory_space=pltpu.VMEM)
    extra = padded(-(-experts // (width // rows)))
    out = jax.ShapeDtypeStruct((ndy * ndx, rows + extra, width), jnp.bfloat16)
    m = ndy * rows
    return pl.pallas_call(
        functools.partial(
            expert_kernel, (at, out_at, len(pieces), ndy, ndx, local, experts, rows, tile, wide)
        ),
        in_specs=[pl.BlockSpec(memory_space=pltpu.SMEM)] + [vmem] * (len(pieces) + 3),
        out_specs=[vmem] * 2,
        scratch_shapes=[pltpu.VMEM((m, units), jnp.bfloat16)] * 2
        + [pltpu.VMEM((padded(local), m), jnp.float32)],
        out_shape=[out] * 2,
        compiler_params=pltpu.CompilerParams(vmem_limit_bytes=16 << 20),
        cost_estimate=pl.CostEstimate(
            flops=10 * m * units * full, bytes_accessed=6 * units * full, transcendentals=0
        ),
    )(where, *pieces, *weights)


def exchange(x, axis, step):
    return lax.ppermute(x, axis, [(i, i ^ step) for i in range(lax.axis_size(axis))])


def passed(x, axis, pairs):
    return lax.ppermute(x, axis, pairs)


def bits(size):
    return [1 << b for b in range(size.bit_length() - 1)]


def last_bit(v):
    return 1 << (v.bit_length() - 1)


def added(a, b):
    return (a.astype(jnp.float32) + b.astype(jnp.float32)).astype(jnp.bfloat16)


class Cell:
    def __init__(self, value):
        self.v = value


def together(cells):
    cells = list({id(c): c for c in cells}.values())
    if len(cells) > 1:
        for c, v in zip(cells, lax.optimization_barrier([c.v for c in cells])):
            c.v = v


def exchange(x, axis, step):
    return lax.ppermute(x, axis, [(i, i ^ step) for i in range(lax.axis_size(axis))])


def passed(x, axis, pairs):
    return lax.ppermute(x, axis, pairs)


def bits(size):
    return [1 << b for b in range(size.bit_length() - 1)]


def last_bit(v):
    return 1 << (v.bit_length() - 1)


def added(a, b):
    return (a.astype(jnp.float32) + b.astype(jnp.float32)).astype(jnp.bfloat16)


class Cell:
    def __init__(self, value):
        self.v = value


def together(cells):
    cells = list({id(c): c for c in cells}.values())
    if len(cells) > 1:
        for c, v in zip(cells, lax.optimization_barrier([c.v for c in cells])):
            c.v = v


def touch_kernel(where, *refs):
    for i in range(where.shape[0]):
        refs[-1][i] = where[i]


def touch_call(where, arrays):
    smem, vmem = pl.BlockSpec(memory_space=pltpu.SMEM), pl.BlockSpec(memory_space=pltpu.VMEM)
    return pl.pallas_call(
        touch_kernel,
        in_specs=[smem] + [vmem] * len(arrays),
        out_specs=smem,
        out_shape=jax.ShapeDtypeStruct(where.shape, where.dtype),
        compiler_params=pltpu.CompilerParams(vmem_limit_bytes=2 << 20),
    )(where, *arrays)


def body(tokens, grad_out, expert_ids, gate_probs, gate_weight, up_weight, down_weight):
    far, near, cols = lax.axis_size("far"), lax.axis_size("near"), lax.axis_size("col")
    z, y, x, c = (lax.axis_index(n) for n in ("far", "near", "col", "half"))
    me = z * near + y
    local, _, full = gate_weight.shape
    weights = [w.reshape(-1, full) for w in (gate_weight, up_weight, down_weight)]
    experts = local * far * near
    rows, width = tokens.shape
    features = [(x ^ dx) * 2 + (c ^ dc) for dx in range(cols) for dc in range(2)]
    where = Cell(jnp.stack([me] + features).astype(jnp.int32))
    labels = [(dy, dx) for dy in range(near) for dx in range(cols)]
    depth = {l: bin(l[0]).count("1") + bin(l[1]).count("1") for l in labels}
    depths = max(depth.values())

    spread = jax.nn.one_hot(expert_ids, experts, dtype=jnp.float32)
    probs = jnp.sum(spread * gate_probs[:, :, None], axis=1).T
    parts = []
    for _ in range(3):
        parts.append(lax.reduce_precision(probs, 8, 7))
        probs = probs - parts[-1]
    table = jnp.concatenate(parts, axis=1).astype(jnp.bfloat16)
    table = jnp.pad(table, ((0, padded(experts) - experts), (0, width - 3 * rows)))

    have = [{} for _ in range(far)]
    have[0][0, 0, 0] = [Cell(jnp.concatenate([tokens, grad_out, table], axis=0))]

    def far_ops(q):
        return [(q, (0, 0, 0), [(c, None) for c in have[0][0, 0, 0]], "far", q)] if 0 < q < far else []

    line = far == 4
    inner = (z == 1) | (z == 2)
    outward, across = [(1, 0), (2, 3)], [(1, 2), (2, 1)]
    held = {}

    def line_sources(r):
        if r == 0:
            return [have[0][0, 0, 0][0]]
        if r == 1:
            return [held["across"], have[1][0, 0, 0][0]]
        return [held["inner"]] if r == 2 else []

    def line_step(r):
        if r == 0:
            own = have[0][0, 0, 0][0].v
            have[1][0, 0, 0] = [Cell(exchange(own, "far", 1))]
            held["across"] = Cell(passed(own, "far", across))
            return [have[1][0, 0, 0][0], held["across"]]
        if r == 1:
            held["outer"] = Cell(passed(held["across"].v, "far", outward))
            held["inner"] = Cell(passed(have[1][0, 0, 0][0].v, "far", across))
            return [held["outer"], held["inner"]]
        if r == 2:
            held["last"] = Cell(passed(held["inner"].v, "far", outward))
            return [held["last"]]
        return []

    def line_arrive(r):
        if r == 2:
            have[2][0, 0, 0] = [Cell(jnp.where(inner, held["inner"].v, held["outer"].v))]
        if r == 3:
            have[3][0, 0, 0] = [Cell(jnp.where(inner, held["across"].v, held["last"].v))]

    def level_ops(q, level):
        ops = []
        for dy, dx in labels:
            if depth[dy, dx] != level:
                continue
            if dy and dx and q % 4 not in (0,2,3,):
                whole = have[q][dy, dx ^ last_bit(dx), 0]
                ops.append((q, (dy, dx, 0), [(c, None) for c in whole], "col", last_bit(dx)))
            elif dy and dx:
                by_near, by_col = have[q][dy ^ last_bit(dy), dx, 0], have[q][dy, dx ^ last_bit(dx), 0]
                t = (by_near[0], (0, rows) if len(by_near) == 1 else None)
                g = (by_col[-1], (rows, 2 * rows) if len(by_col) == 1 else None)
                ops.append((q, (dy, dx, 0), [t], "near", last_bit(dy)))
                ops.append((q, (dy, dx, 0), [g], "col", last_bit(dx)))
            elif dy:
                whole = have[q][dy ^ last_bit(dy), dx, 0]
                ops.append((q, (dy, dx, 0), [(c, None) for c in whole], "near", last_bit(dy)))
            else:
                whole = have[q][dy, dx ^ last_bit(dx), 0]
                ops.append((q, (dy, dx, 0), [(c, None) for c in whole], "col", last_bit(dx)))
        return ops

    def half_ops(q, level):
        return [
            (q, (dy, dx, 1), [(c, None) for c in have[q][dy, dx, 0]], "half", 1)
            for dy, dx in labels
            if depth[dy, dx] == level
        ]

    def compute(q):
        pieces, at = [], {}
        for l, cells in have[q].items():
            first = len(pieces)
            pieces += [c.v for c in cells]
            at[(0,) + l] = (first, 0)
            at[(1,) + l] = (first, rows) if len(cells) == 1 else (first + 1, 0)
            at[(2,) + l] = (first, 2 * rows)
        out_at = {(dy, dx): dy * cols + dx for dy, dx in labels}
        return expert_call(where, pieces, weights, local, experts, rows, at, out_at, near, cols)

    class Sum:
        def __init__(self, q, keep, send):
            self.q, self.half, self.todo, self.mine = q, None, None, None
            self.cells = [Cell(keep), Cell(send)]
            self.urgent = q > 0
            self.orders = [("near", "col"), ("col", "near")]

        def begin(self):
            self.half = Cell(exchange(self.cells[1].v, "half", 1))

        def first(self):
            keep = self.cells[0].v
            shape = (near, cols) + keep.shape[1:]
            part = shape[2] // len(self.orders)
            keep, got = keep.reshape(shape), self.half.v.reshape(shape)
            cut = lambda x: [x[:, :, i * part : (i + 1) * part] for i in range(len(self.orders))]
            self.todo = [
                [(a, s) for a in o for s in reversed(bits(near if a == "near" else cols))] for o in self.orders
            ]
            self.fold(cut(keep), cut(got))

        def left(self):
            return len(self.todo[0])

        def fold(self, keep, got):
            self.keep, self.send = [], []
            for k, g, todo in zip(keep, got, self.todo):
                dim = 0 if todo[0][0] == "near" else 1
                (k0, k1), (g0, g1) = jnp.split(k, 2, axis=dim), jnp.split(g, 2, axis=dim)
                self.send.append(Cell(added(k1, g1)))
                self.keep.append(Cell(added(k0, g0)))

        def step(self):
            self.got = [Cell(exchange(s.v, *todo.pop(0))) for s, todo in zip(self.send, self.todo)]
            return self.got

        def refold(self):
            self.fold([c.v for c in self.keep], [c.v for c in self.got])

        def finish(self):
            mine = [added(k.v, g.v)[0, 0] for k, g in zip(self.keep, self.got)]
            self.mine = Cell(mine[0] if len(mine) == 1 else jnp.concatenate(mine, axis=0))

        def home(self):
            homes.append(Cell(exchange(self.mine.v, "far", self.q) if self.q else self.mine.v))
            sums.remove(self)

    where = where.v
    ready, sums, homes, held_back = [], [], [], []
    r = 0
    while r < far + depths or sums:
        if line and r:
            together(ready + line_sources(r))
            line_arrive(r)
        ops = []
        for q in range(far):
            if 0 <= r - q < depths:
                ops += level_ops(q, r - q + 1)
        ops += [] if line else far_ops(r + 1)
        for q in range(far):
            if 0 <= r - q <= depths:
                ops += half_ops(q, r - q)
        if r and not line:
            together(ready + [c for o in ops for c, _ in o[2]])
        ready = line_step(r) if line else []
        working = r - depths if 0 <= r - depths < far else None
        begun = []
        for s in list(sums):
            if s.half is None:
                s.begin()
                if s.urgent:
                    s.first()
                    begun.append(s)
                else:
                    ready.append(s.half)
            elif s.todo is None:
                if r >= depths + 4:
                    s.first()
                    ready += s.step()
                else:
                    ready.append(s.half)
            elif s.left() == 1 and not s.urgent and any(o.urgent and (o.todo is None or o.left()) for o in sums):
                ready += s.got
            elif s.left():
                s.refold()
                ready += s.step()
            elif s.mine is None:
                s.finish()
                s.home()
        for q, label, sources, axis, bit in ops:
            for c, cut in sources:
                got = Cell(exchange(c.v if cut is None else c.v[cut[0] : cut[1]], axis, bit))
                have[q].setdefault(label, []).append(got)
                if axis != "half":
                    ready.append(got)
        if begun and working is not None:
            together([c for s in begun for c in s.send] + have[working][0, 0, 0])
        for s in begun:
            ready += s.step()
        ready, held_back = ready + held_back, []
        if begun and working is None:
            for s in [s for s in sums if s.q == far - 2 and not s.left()]:
                s.finish()
                s.home()
                held_back.append(homes[-1])
        if working is not None:
            s = Sum(working, *compute(working))
            sums.append(s)
            ready += s.cells
        r += 1
    total = sum(h.v.astype(jnp.float32) for h in homes)

    grad_tokens = total[:rows].astype(jnp.bfloat16)
    by_expert = total[rows:].reshape(-1, rows)[:experts]
    grad_gates = jnp.sum(spread * by_expert.T[:, None, :], axis=2)
    return (grad_tokens, grad_gates.astype(jnp.bfloat16))


def solution(mesh):
    expert, ctx = mesh.shape["expert"], mesh.shape["ctx"]
    fine = Mesh(mesh.devices.reshape(expert // 2, 2, ctx // 2, 2), ("far", "near", "col", "half"))
    e, c = ("far", "near"), ("col", "half")
    return jax.shard_map(
        body,
        mesh=fine,
        in_specs=(P(e, c), P(e, c), P(e), P(e), P(e, c), P(e, c), P(e, c)),
        out_specs=(P(e, c), P(e)),
        check_vma=False,
    )
```

```python
import functools
import jax
import jax.numpy as jnp
from jax import lax
from jax.experimental import pallas as pl
from jax.experimental.pallas import tpu as pltpu
from jax.sharding import Mesh, PartitionSpec as P

NT = (((1,), (1,)), ((), ()))
NN = (((1,), (0,)), ((), ()))
TN = (((0,), (0,)), ((), ()))


def padded(count):
    return 16 * -(-count // 16)


def expert_kernel(plan, *refs):
    at, out_at, n_in, ndy, ndx, local, experts, rows, tile, wide, bring = plan
    where = refs[0]
    pieces = refs[1 : 1 + n_in]
    given, (keep, send) = refs[1 + n_in : 4 + n_in], refs[4 + n_in : 6 + n_in]
    if bring:
        wg, wu, wd, d_gate, d_up, score, arrived = refs[6 + n_in :]
    else:
        (wg, wu, wd), (d_gate, d_up, score) = given, refs[6 + n_in :]
    width = pieces[0].shape[1]
    units = wg.shape[0]
    hidden = units // local
    blocks = [(dx, dc) for dx in range(ndx) for dc in range(2)]

    def feature(dx, dc):
        return pl.multiple_of(where[1 + 2 * dx + dc] * width, width)

    def part(kind, dy, dx, dc):
        ref, first = at[kind, dy, dx, dc]
        return pieces[ref][first : first + rows]

    def product(kind, ref, first):
        total = None
        for dx, dc in blocks:
            x = jnp.concatenate([part(kind, dy, dx, dc) for dy in range(ndy)], axis=0)
            w = ref[pl.ds(first, tile), pl.ds(feature(dx, dc), width)]
            term = lax.dot_general(x, w, NT, preferred_element_type=jnp.float32)
            total = term if total is None else total + term
        return total

    def weight_copy(k, n):
        part = pl.ds(pl.multiple_of(n * tile, tile), tile)
        return pltpu.make_async_copy(given[k].at[part], (wg, wu, wd)[k].at[part], arrived.at[k, n])

    if bring:
        for k in range(3):
            weight_copy(k, 0).start()

    slots = padded(experts)
    expert = lax.broadcasted_iota(jnp.int32, (slots, 128), 0)
    column = lax.broadcasted_iota(jnp.int32, (slots, 128), 1)
    mine = jnp.where((expert == where[0] * local + column) & (column < local), 1.0, 0.0).astype(jnp.bfloat16)
    shares = []
    for dy in range(ndy):
        ref, first = at[2, dy, 0, 0]
        table = pieces[ref][first : first + slots]
        shares.append(
            sum(
                lax.dot_general(
                    table[:, i * rows : (i + 1) * rows], mine, TN, preferred_element_type=jnp.float32
                )
                for i in range(3)
            )
        )
    shares = jnp.concatenate(shares, axis=0)
    score[...] = jnp.zeros(score.shape, jnp.float32)

    @pl.loop(0, units // tile)
    def _(n):
        first = pl.multiple_of(n * tile, tile)
        if bring:
            weight_copy(0, n).wait()

            @pl.when(n + 1 < units // tile)
            def _():
                for k in range(3):
                    weight_copy(k, n + 1).start()

        gate = product(0, wg, first)
        if bring:
            weight_copy(1, n).wait()
        up = product(0, wu, first)
        if bring:
            weight_copy(2, n).wait()
        hid = product(1, wd, first)
        unit = first + lax.broadcasted_iota(jnp.int32, gate.shape, 1)
        share = jnp.zeros(gate.shape, jnp.float32)
        sig = jax.nn.sigmoid(gate)
        act = gate * sig
        both = up * hid
        scores = act * both
        for e in range(local):
            inside = (unit >= e * hidden) & (unit < (e + 1) * hidden)
            share = jnp.where(inside, shares[:, e : e + 1], share)
        row = lax.broadcasted_iota(jnp.int32, (score.shape[0], tile), 0) * hidden
        of = first + lax.broadcasted_iota(jnp.int32, (score.shape[0], tile), 1)
        pick = jnp.where((of >= row) & (of < row + hidden), 1.0, 0.0).astype(jnp.bfloat16)
        high = scores.astype(jnp.bfloat16)
        low = (scores - high.astype(jnp.float32)).astype(jnp.bfloat16)
        score[...] += lax.dot_general(pick, high, NT, preferred_element_type=jnp.float32) + lax.dot_general(
            pick, low, NT, preferred_element_type=jnp.float32
        )
        d_gate[:, pl.ds(first, tile)] = (share * (both * sig * (1.0 + gate * (1.0 - sig)))).astype(
            jnp.bfloat16
        )
        d_up[:, pl.ds(first, tile)] = (share * (hid * act)).astype(jnp.bfloat16)

    extra = keep.shape[1] - rows
    per_row = width // rows
    place = lax.broadcasted_iota(jnp.int32, (extra, width), 0) * per_row
    place = place + lax.broadcasted_iota(jnp.int32, (extra, width), 1) // rows
    for dy in range(ndy):
        table = jnp.zeros((extra, width), jnp.float32)
        for e in range(local):
            line = jnp.concatenate([score[e : e + 1, dy * rows : (dy + 1) * rows]] * per_row, axis=1)
            table = jnp.where(place == where[0] * local + e, line, table)
        for dx, dc in blocks:
            (keep, send)[dc][out_at[dy, dx], rows:, :] = table.astype(jnp.bfloat16)

    for dx, dc in blocks:

        @pl.loop(0, width // wide)
        def _(n):
            start = pl.multiple_of(n * wide, wide)
            source = pl.ds(pl.multiple_of(feature(dx, dc) + start, wide), wide)
            total = lax.dot_general(
                d_gate[...], wg[:, source], NN, preferred_element_type=jnp.float32
            ) + lax.dot_general(d_up[...], wu[:, source], NN, preferred_element_type=jnp.float32)
            total = total.astype(jnp.bfloat16)
            for dy in range(ndy):
                (keep, send)[dc][out_at[dy, dx], :rows, pl.ds(start, wide)] = total[dy * rows : (dy + 1) * rows]


def expert_call(where, pieces, weights, local, experts, rows, at, out_at, ndy, ndx, bring):
    units, full = weights[0].shape
    width = pieces[0].shape[1]
    tile = next(t for t in (256, 128, 64, 32, 16) if units % t == 0)
    wide = next(t for t in (1024, 512, 256, 128) if width % t == 0)
    vmem = pl.BlockSpec(memory_space=pltpu.VMEM)
    if bring:
        weights = [pltpu.with_memory_space_constraint(w, pltpu.HBM) for w in weights]
    extra = padded(-(-experts // (width // rows)))
    out = jax.ShapeDtypeStruct((ndy * ndx, rows + extra, width), jnp.bfloat16)
    m = ndy * rows
    return pl.pallas_call(
        functools.partial(
            expert_kernel, (at, out_at, len(pieces), ndy, ndx, local, experts, rows, tile, wide, bring)
        ),
        in_specs=[pl.BlockSpec(memory_space=pltpu.SMEM)] + [vmem] * len(pieces)
        + [pl.BlockSpec(memory_space=pltpu.HBM) if bring else vmem] * 3,
        out_specs=[vmem] * (5 if bring else 2),
        scratch_shapes=[pltpu.VMEM((m, units), jnp.bfloat16)] * 2
        + [pltpu.VMEM((padded(local), m), jnp.float32)]
        + [pltpu.SemaphoreType.DMA((3, units // tile))] * bring,
        out_shape=[out] * 2 + [jax.ShapeDtypeStruct(w.shape, w.dtype) for w in weights] * bring,
        compiler_params=pltpu.CompilerParams(vmem_limit_bytes=16 << 20),
        cost_estimate=pl.CostEstimate(
            flops=10 * m * units * full, bytes_accessed=6 * units * full, transcendentals=0
        ),
    )(where, *pieces, *weights)


def exchange(x, axis, step):
    return lax.ppermute(x, axis, [(i, i ^ step) for i in range(lax.axis_size(axis))])


def passed(x, axis, pairs):
    return lax.ppermute(x, axis, pairs)


def bits(size):
    return [1 << b for b in range(size.bit_length() - 1)]


def last_bit(v):
    return 1 << (v.bit_length() - 1)


def added(a, b):
    return (a.astype(jnp.float32) + b.astype(jnp.float32)).astype(jnp.bfloat16)


class Cell:
    def __init__(self, value):
        self.v = value


def together(cells):
    cells = list({id(c): c for c in cells}.values())
    if len(cells) > 1:
        for c, v in zip(cells, lax.optimization_barrier([c.v for c in cells])):
            c.v = v


def exchange(x, axis, step):
    return lax.ppermute(x, axis, [(i, i ^ step) for i in range(lax.axis_size(axis))])


def passed(x, axis, pairs):
    return lax.ppermute(x, axis, pairs)


def bits(size):
    return [1 << b for b in range(size.bit_length() - 1)]


def last_bit(v):
    return 1 << (v.bit_length() - 1)


def added(a, b):
    return (a.astype(jnp.float32) + b.astype(jnp.float32)).astype(jnp.bfloat16)


class Cell:
    def __init__(self, value):
        self.v = value


def together(cells):
    cells = list({id(c): c for c in cells}.values())
    if len(cells) > 1:
        for c, v in zip(cells, lax.optimization_barrier([c.v for c in cells])):
            c.v = v


def touch_kernel(where, *refs):
    for i in range(where.shape[0]):
        refs[-1][i] = where[i]


def touch_call(where, arrays):
    smem, vmem = pl.BlockSpec(memory_space=pltpu.SMEM), pl.BlockSpec(memory_space=pltpu.VMEM)
    return pl.pallas_call(
        touch_kernel,
        in_specs=[smem] + [vmem] * len(arrays),
        out_specs=smem,
        out_shape=jax.ShapeDtypeStruct(where.shape, where.dtype),
        compiler_params=pltpu.CompilerParams(vmem_limit_bytes=2 << 20),
    )(where, *arrays)


def body(tokens, grad_out, expert_ids, gate_probs, gate_weight, up_weight, down_weight):
    far, near, cols = lax.axis_size("far"), lax.axis_size("near"), lax.axis_size("col")
    z, y, x, c = (lax.axis_index(n) for n in ("far", "near", "col", "half"))
    me = z * near + y
    local, _, full = gate_weight.shape
    weights = [w.reshape(-1, full) for w in (gate_weight, up_weight, down_weight)]
    experts = local * far * near
    rows, width = tokens.shape
    features = [(x ^ dx) * 2 + (c ^ dc) for dx in range(cols) for dc in range(2)]
    where = Cell(jnp.stack([me] + features).astype(jnp.int32))
    labels = [(dy, dx) for dy in range(near) for dx in range(cols)]
    depth = {l: bin(l[0]).count("1") + bin(l[1]).count("1") for l in labels}
    depths = max(depth.values())

    spread = jax.nn.one_hot(expert_ids, experts, dtype=jnp.float32)
    probs = jnp.sum(spread * gate_probs[:, :, None], axis=1).T
    parts = []
    for _ in range(3):
        parts.append(lax.reduce_precision(probs, 8, 7))
        probs = probs - parts[-1]
    table = jnp.concatenate(parts, axis=1).astype(jnp.bfloat16)
    table = jnp.pad(table, ((0, padded(experts) - experts), (0, width - 3 * rows)))

    have = [{} for _ in range(far)]
    have[0][0, 0, 0] = [Cell(jnp.concatenate([tokens, grad_out, table], axis=0))]

    def far_ops(q):
        return [(q, (0, 0, 0), [(c, None) for c in have[0][0, 0, 0]], "far", q)] if 0 < q < far else []

    line = far == 4
    inner = (z == 1) | (z == 2)
    outward, across = [(1, 0), (2, 3)], [(1, 2), (2, 1)]
    held = {}

    def line_sources(r):
        if r == 0:
            return [have[0][0, 0, 0][0]]
        if r == 1:
            return [held["across"], have[1][0, 0, 0][0]]
        return [held["inner"]] if r == 2 else []

    def line_step(r):
        if r == 0:
            own = have[0][0, 0, 0][0].v
            have[1][0, 0, 0] = [Cell(exchange(own, "far", 1))]
            held["across"] = Cell(passed(own, "far", across))
            return [have[1][0, 0, 0][0], held["across"]]
        if r == 1:
            held["outer"] = Cell(passed(held["across"].v, "far", outward))
            held["inner"] = Cell(passed(have[1][0, 0, 0][0].v, "far", across))
            return [held["outer"], held["inner"]]
        if r == 2:
            held["last"] = Cell(passed(held["inner"].v, "far", outward))
            return [held["last"]]
        return []

    def line_arrive(r):
        if r == 2:
            have[2][0, 0, 0] = [Cell(jnp.where(inner, held["inner"].v, held["outer"].v))]
        if r == 3:
            have[3][0, 0, 0] = [Cell(jnp.where(inner, held["across"].v, held["last"].v))]

    def level_ops(q, level):
        ops = []
        for dy, dx in labels:
            if depth[dy, dx] != level:
                continue
            if dy and dx and q % 4 not in (0,2,3,):
                whole = have[q][dy, dx ^ last_bit(dx), 0]
                ops.append((q, (dy, dx, 0), [(c, None) for c in whole], "col", last_bit(dx)))
            elif dy and dx:
                by_near, by_col = have[q][dy ^ last_bit(dy), dx, 0], have[q][dy, dx ^ last_bit(dx), 0]
                t = (by_near[0], (0, rows) if len(by_near) == 1 else None)
                g = (by_col[-1], (rows, 2 * rows) if len(by_col) == 1 else None)
                ops.append((q, (dy, dx, 0), [t], "near", last_bit(dy)))
                ops.append((q, (dy, dx, 0), [g], "col", last_bit(dx)))
            elif dy:
                whole = have[q][dy ^ last_bit(dy), dx, 0]
                ops.append((q, (dy, dx, 0), [(c, None) for c in whole], "near", last_bit(dy)))
            else:
                whole = have[q][dy, dx ^ last_bit(dx), 0]
                ops.append((q, (dy, dx, 0), [(c, None) for c in whole], "col", last_bit(dx)))
        return ops

    def half_ops(q, level):
        return [
            (q, (dy, dx, 1), [(c, None) for c in have[q][dy, dx, 0]], "half", 1)
            for dy, dx in labels
            if depth[dy, dx] == level
        ]

    brought = []

    def compute(q):
        pieces, at = [], {}
        for l, cells in have[q].items():
            first = len(pieces)
            pieces += [c.v for c in cells]
            at[(0,) + l] = (first, 0)
            at[(1,) + l] = (first, rows) if len(cells) == 1 else (first + 1, 0)
            at[(2,) + l] = (first, 2 * rows)
        out_at = {(dy, dx): dy * cols + dx for dy, dx in labels}
        bring = not brought
        results = expert_call(
            where, pieces, brought or weights, local, experts, rows, at, out_at, near, cols, bring
        )
        brought.extend(results[2:])
        return results[:2]

    class Sum:
        def __init__(self, q, keep, send):
            self.q, self.half, self.todo, self.mine = q, None, None, None
            self.cells = [Cell(keep), Cell(send)]
            self.urgent = q > 0
            self.orders = [("near", "col"), ("col", "near")]

        def begin(self):
            self.half = Cell(exchange(self.cells[1].v, "half", 1))

        def first(self):
            keep = self.cells[0].v
            shape = (near, cols) + keep.shape[1:]
            part = shape[2] // len(self.orders)
            keep, got = keep.reshape(shape), self.half.v.reshape(shape)
            cut = lambda x: [x[:, :, i * part : (i + 1) * part] for i in range(len(self.orders))]
            self.todo = [
                [(a, s) for a in o for s in reversed(bits(near if a == "near" else cols))] for o in self.orders
            ]
            self.fold(cut(keep), cut(got))

        def left(self):
            return len(self.todo[0])

        def fold(self, keep, got):
            self.keep, self.send = [], []
            for k, g, todo in zip(keep, got, self.todo):
                dim = 0 if todo[0][0] == "near" else 1
                (k0, k1), (g0, g1) = jnp.split(k, 2, axis=dim), jnp.split(g, 2, axis=dim)
                self.send.append(Cell(added(k1, g1)))
                self.keep.append(Cell(added(k0, g0)))

        def step(self):
            self.got = [Cell(exchange(s.v, *todo.pop(0))) for s, todo in zip(self.send, self.todo)]
            return self.got

        def refold(self):
            self.fold([c.v for c in self.keep], [c.v for c in self.got])

        def finish(self):
            mine = [added(k.v, g.v)[0, 0] for k, g in zip(self.keep, self.got)]
            self.mine = Cell(mine[0] if len(mine) == 1 else jnp.concatenate(mine, axis=0))

        def home(self):
            homes.append(Cell(exchange(self.mine.v, "far", self.q) if self.q else self.mine.v))
            sums.remove(self)

    where = where.v
    ready, sums, homes, held_back = [], [], [], []
    r = 0
    while r < far + depths or sums:
        if line and r:
            together(ready + line_sources(r))
            line_arrive(r)
        ops = []
        for q in range(far):
            if 0 <= r - q < depths:
                ops += level_ops(q, r - q + 1)
        ops += [] if line else far_ops(r + 1)
        for q in range(far):
            if 0 <= r - q <= depths:
                ops += half_ops(q, r - q)
        if r and not line:
            together(ready + [c for o in ops for c, _ in o[2]])
        ready = line_step(r) if line else []
        working = r - depths if 0 <= r - depths < far else None
        begun = []
        for s in list(sums):
            if s.half is None:
                s.begin()
                if s.urgent:
                    s.first()
                    begun.append(s)
                else:
                    ready.append(s.half)
            elif s.todo is None:
                if r >= depths + 4:
                    s.first()
                    ready += s.step()
                else:
                    ready.append(s.half)
            elif s.left() == 1 and not s.urgent and any(o.urgent and (o.todo is None or o.left()) for o in sums):
                ready += s.got
            elif s.left():
                s.refold()
                ready += s.step()
            elif s.mine is None:
                s.finish()
                s.home()
        for q, label, sources, axis, bit in ops:
            for c, cut in sources:
                got = Cell(exchange(c.v if cut is None else c.v[cut[0] : cut[1]], axis, bit))
                have[q].setdefault(label, []).append(got)
                if axis != "half":
                    ready.append(got)
        if begun and working is not None:
            together([c for s in begun for c in s.send] + have[working][0, 0, 0])
        for s in begun:
            ready += s.step()
        ready, held_back = ready + held_back, []
        if begun and working is None:
            for s in [s for s in sums if s.q == far - 2 and not s.left()]:
                s.finish()
                s.home()
                held_back.append(homes[-1])
        if working is not None:
            s = Sum(working, *compute(working))
            sums.append(s)
            ready += s.cells
        r += 1
    total = sum(h.v.astype(jnp.float32) for h in homes)

    grad_tokens = total[:rows].astype(jnp.bfloat16)
    by_expert = total[rows:].reshape(-1, rows)[:experts]
    grad_gates = jnp.sum(spread * by_expert.T[:, None, :], axis=2)
    return (grad_tokens, grad_gates.astype(jnp.bfloat16))


def solution(mesh):
    expert, ctx = mesh.shape["expert"], mesh.shape["ctx"]
    fine = Mesh(mesh.devices.reshape(expert // 2, 2, ctx // 2, 2), ("far", "near", "col", "half"))
    e, c = ("far", "near"), ("col", "half")
    return jax.shard_map(
        body,
        mesh=fine,
        in_specs=(P(e, c), P(e, c), P(e), P(e), P(e, c), P(e, c), P(e, c)),
        out_specs=(P(e, c), P(e)),
        check_vma=False,
    )
```
